512 devices in a mesh: user: 64 (over z, y), item: 8 (over x, core).
Axes of the slice: x: 4, y: 8, z: 8, core: 2. Of those that a mesh axis runs over, the one named last changes fastest.
Arguments:
- tile_values: bfloat16 [7168, 1024, 128], P('user', 'item')
- tile_coords: int32 [7168, 16], P('user', 'item'), may hold values from 0 to 31, as said below
- tile_counts: int32 [64, 8], P('user', 'item'), may hold values from 28 to 112, as said below
- omega: bfloat16 [32768, 128], P('item')
Outputs:
- scaled_q: float32 [262144, 128], P(('user', 'item'))
- scaled_r: float32 [128, 128], replicated
- first_r: float32 [128, 128], replicated
The draws below stay inside these ranges and needn't reach their ends.
Inputs may be any that keep to these rules, and one draw needn't show every extreme that they name: `tile_coords`: within one device block the slots name distinct tiles; the first of a pair is below 32, the second below 32; slots at or past the block's count are not part of A. `tile_counts`: some device block uses all 112 slots.
All inputs are finite; a program needn't handle non-finite values.
Results may differ from the reference program's by a relative error of at most 0.00035.
Values may be sent and summed in bfloat16 or wider, within the bound.
No kernel may reach another device: no remote copies, remote signals or barrier semaphores. Data moves between devices by JAX's collectives and lax.ppermute only.
A program may use at most 64 MiB of HBM per device.

```python
import math
import jax
import jax.numpy as jnp
from jax import lax

TILE = 128
K = 128
RB = 32
CB = 32
SLOTS = 112
ROWS = 262144
COLS = 32768


def tile_pairs(key):
    key = jax.random.fold_in(key, 23)
    users = ROWS // (RB * TILE)
    items = COLS // (CB * TILE)
    keys = jax.random.split(key, users * items)
    perms = jax.vmap(lambda k: jax.random.permutation(k, RB * CB))(keys)[:, :SLOTS]
    perms = perms.reshape(users, items, SLOTS).astype(jnp.int32)
    pairs = jnp.stack([perms // CB, perms % CB], axis=-1)
    pairs = jnp.transpose(pairs, (0, 2, 1, 3))
    return pairs.reshape(users * SLOTS, items * 2).astype(jnp.int32)


def column_weights(key):
    key = jax.random.fold_in(key, 53)
    ranking = jax.random.permutation(key, COLS).astype(jnp.int32)
    return jnp.where(ranking < K // 2, 1.0, 1000.0).astype(jnp.float32)


def draw_tile_values(key, part):
    pairs = tile_pairs(key)
    weights = column_weights(key)
    key = jax.random.fold_in(key, 11)
    users = ROWS // (RB * TILE)
    items = COLS // (CB * TILE)
    shape = (users * SLOTS, items * TILE, TILE)
    position = (jnp.arange(users * SLOTS, dtype=jnp.int32) // SLOTS).astype(jnp.float32)
    fraction = (position / max(users - 1, 1)).reshape(users * SLOTS, 1, 1)
    values = jax.random.normal(key, shape, jnp.float32) * jnp.sqrt(1.0 + 4.0 * fraction)
    col_tiles = pairs.reshape(users * SLOTS, items, 2)[:, :, 1]
    starts = (jnp.arange(items, dtype=jnp.int32)[None, :] * CB + col_tiles) * TILE
    columns_at = starts[:, :, None] + jnp.arange(TILE, dtype=jnp.int32)[None, None, :]
    scales = weights[columns_at].reshape(users * SLOTS, items, 1, TILE)
    values = (values.reshape(users * SLOTS, items, TILE, TILE) * scales).reshape(shape)
    return values.astype(jnp.bfloat16)


def draw_tile_coords(key, part):
    return tile_pairs(key)


def draw_tile_counts(key, part):
    key = jax.random.fold_in(key, 37)
    users = ROWS // (RB * TILE)
    items = COLS // (CB * TILE)
    first, second = jax.random.split(key)
    raw = jax.random.randint(first, (users * items,), 0, SLOTS + 1, dtype=jnp.int32)
    counts = jnp.maximum(SLOTS // 4, raw * raw // SLOTS)
    chosen = jax.random.randint(second, (), 0, users * items, dtype=jnp.int32)
    counts = jnp.where(jnp.arange(users * items, dtype=jnp.int32) == chosen, SLOTS, counts)
    return counts.reshape(users, items).astype(jnp.int32)


def draw_omega(key, part):
    weights = column_weights(key)
    key = jax.random.fold_in(key, 41)
    items = COLS // (CB * TILE)
    fan = TILE * SLOTS * items / (2.0 * RB)
    first, second, third = jax.random.split(key, 3)
    spread = jnp.exp(jax.random.uniform(third, (1, K), jnp.float32, math.log(0.012), math.log(0.04)))
    common = jnp.clip(jax.random.normal(first, (COLS, 1), jnp.float32), -5.0, 5.0)
    own = jnp.clip(jax.random.normal(second, (COLS, K), jnp.float32), -5.0, 5.0)
    values = common + spread * own
    values = values / weights[:, None]
    return (values / math.sqrt(fan)).astype(jnp.bfloat16)


def setup_inputs(seed: int = 0) -> dict:
    splits = jax.random.split(jax.random.key(seed), 5)
    return {
        "tile_values": draw_tile_values(jax.random.fold_in(splits[4], 71), 0),
        "tile_coords": draw_tile_coords(jax.random.fold_in(splits[4], 71), 0),
        "tile_counts": draw_tile_counts(jax.random.fold_in(splits[4], 71), 0),
        "omega": draw_omega(jax.random.fold_in(splits[4], 71), 0),
    }


def right_solve(lower, rows):
    return lax.linalg.triangular_solve(lower, rows, left_side=False, lower=True, transpose_a=True)

def cholesky_qr(sketch):
    gram_one = jnp.einsum('rk,rl->kl', sketch, sketch, precision=lax.Precision.HIGHEST)
    lower_one = jnp.linalg.cholesky(gram_one)
    basis_one = right_solve(lower_one, sketch)
    gram_two = jnp.einsum('rk,rl->kl', basis_one, basis_one, precision=lax.Precision.HIGHEST)
    lower_two = jnp.linalg.cholesky(gram_two)
    basis = right_solve(lower_two, basis_one)
    factor = jnp.dot(lower_two.T, lower_one.T, precision=lax.Precision.HIGHEST)
    return (basis, factor, lower_one)

def reference(tile_values, tile_coords, tile_counts, omega):
    users = ROWS // (RB * TILE)
    items = COLS // (CB * TILE)
    values = tile_values.reshape(users, SLOTS, items, TILE, TILE)
    coords = tile_coords.reshape(users, SLOTS, items, 2)
    blocks = omega.reshape(items, CB, TILE, K).astype(jnp.float32)
    slot_ids = jnp.arange(SLOTS, dtype=jnp.int32)
    row_ids = jnp.arange(RB, dtype=jnp.int32)

    def one_item(tiles, places, count, block):
        chosen = block[places[:, 1]]
        product = jnp.einsum('sij,sjk->sik', tiles.astype(jnp.float32), chosen, precision=lax.Precision.HIGHEST)
        live = (slot_ids < count).astype(jnp.float32)
        onehot = (places[:, 0][:, None] == row_ids[None, :]).astype(jnp.float32) * live[:, None]
        return jnp.einsum('sr,sik->rik', onehot, product, precision=lax.Precision.HIGHEST)

    def one_user(carry, pieces):
        tiles, places, counts = pieces
        parts = jax.vmap(one_item, in_axes=(1, 1, 0, 0))(tiles, places, counts, blocks)
        return (carry, lax.optimization_barrier(jnp.sum(parts, axis=0)).reshape(RB * TILE, K))
    _, sketch = lax.scan(one_user, jnp.zeros((), jnp.float32), (values, coords, tile_counts))
    sketch = sketch.reshape(ROWS, K)
    basis, factor, lower_one = cholesky_qr(sketch)
    scale = jnp.sqrt(jnp.float32(ROWS))
    return (basis * scale, factor / scale, lower_one.T / scale)
```

```python
import jax
import jax.numpy as jnp
from jax import lax
from jax.experimental import pallas as pl
from jax.experimental.pallas import tpu as pltpu
from jax.sharding import Mesh, PartitionSpec as P

RB = 32
HALF = RB // 2
GROUP = 8
ROWS = "z", "y"
COLUMNS = "x", "core"
F32 = jnp.float32
HIGHEST = lax.Precision.HIGHEST
VMEM = pl.BlockSpec(memory_space=pltpu.VMEM)
SMEM = pl.BlockSpec(memory_space=pltpu.SMEM)
ANY = pl.BlockSpec(memory_space=pl.ANY)


def params(mib):
    return pltpu.CompilerParams(vmem_limit_bytes=mib * 2**20)


def mm(a, b, contract=(1, 0)):
    return lax.dot_general(
        a,
        b,
        (((contract[0],), (contract[1],)), ((), ())),
        precision=HIGHEST,
        preferred_element_type=F32,
    )


def two_sum(a, b):
    total = a + b
    other = total - a
    return total, (a - (total - other)) + (b - other)


def sketch_kernel(coords, count, core, tiles, omega, keep, give, held, products, total, fetched, sent):
    tile = held.shape[1]
    used = count[0, 0]
    groups = lax.div(used + (GROUP - 1), GROUP)
    mine = core[0]

    def fetch(g):
        part = pl.ds(pl.multiple_of(g * GROUP, GROUP), GROUP)
        return pltpu.make_async_copy(tiles.at[part], held.at[part], fetched.at[g])

    @pl.loop(0, groups)
    def _(g):
        fetch(g).start()

    total[...] = jnp.zeros_like(total)

    @pl.loop(0, groups)
    def _(g):
        fetch(g).wait()
        for u in range(GROUP):
            s = g * GROUP + u
            column = jnp.clip(coords[s, 1], 0, omega.shape[0] // tile - 1)
            block = omega[pl.ds(pl.multiple_of(column * tile, tile), tile), :]
            products[u] = jnp.dot(held[s], block, preferred_element_type=F32)
        for u in range(GROUP):
            s = g * GROUP + u
            row = coords[s, 0]
            x, rest = lax.div(row, 8), lax.rem(row, 8)
            other = (lax.div(rest, 4) != mine).astype(jnp.int32)
            place = other * HALF + x * 4 + lax.rem(rest, 4)
            place = jnp.where(s < used, jnp.clip(place, 0, RB - 1), RB)
            total[place] += products[u]

    out = [
        pltpu.make_async_copy(total.at[pl.ds(HALF, HALF)], give, sent.at[0]),
        pltpu.make_async_copy(total.at[pl.ds(0, HALF)], keep, sent.at[1]),
    ]
    for copy in out:
        copy.start()
    for copy in out:
        copy.wait()


def partial_sketch(tile_values, tile_coords, tile_counts, omega):
    slots, tile, _ = tile_values.shape
    width = omega.shape[1]
    half = jax.ShapeDtypeStruct((HALF, tile, width), F32)
    core = lax.axis_index("core").astype(jnp.int32).reshape(1)
    return pl.pallas_call(
        sketch_kernel,
        out_shape=(half, half),
        in_specs=[SMEM, SMEM, SMEM, ANY, VMEM],
        out_specs=(ANY, ANY),
        scratch_shapes=[
            pltpu.VMEM((slots, tile, tile), jnp.bfloat16),
            pltpu.VMEM((GROUP, tile, width), F32),
            pltpu.VMEM((RB + 1, tile, width), F32),
            pltpu.SemaphoreType.DMA((slots // GROUP,)),
            pltpu.SemaphoreType.DMA((2,)),
        ],
        compiler_params=params(32),
        name="sketch",
    )(tile_coords, tile_counts, core, tile_values, omega)


SLICES = 4
BITS = 8


def sliced(x, axis, count):
    grid = jnp.max(jnp.abs(x), axis=axis, keepdims=True) * (2.0**17)
    parts = []
    for _ in range(count):
        part = ((x + grid) - grid).astype(jnp.bfloat16)
        x = x - part.astype(F32)
        grid = grid * (2.0**-BITS)
        parts.append(part)
    return parts


def pair_of(orders):
    high, low = orders[0], jnp.zeros_like(orders[0])
    for term in orders[1:]:
        high, error = two_sum(high, term)
        low = low + error
    return two_sum(high, low)


def gram_kernel(pieces, sketch, pairs):
    rows, width = sketch.shape
    x = (pieces[0] + pieces[1]) + (pieces[2] + pieces[3])
    sketch[...] = x
    parts = sliced(x, 0, SLICES)
    across = jnp.concatenate(parts, axis=1)
    orders = [None] * (SLICES + 2)
    for i in range(SLICES):
        reach = min(SLICES, SLICES + 1 - i)
        block = lax.dot_general(
            parts[i],
            across[:, : reach * width],
            (((0,), (0,)), ((), ())),
            preferred_element_type=F32,
        )
        for j in range(reach):
            term = block[:, j * width : (j + 1) * width]
            o = i + j
            orders[o] = term if orders[o] is None else orders[o] + term
    high, low = pair_of([o for o in orders if o is not None])
    h = width // 2
    pairs[pl.ds(0, h, 4), :] = high[:h]
    pairs[pl.ds(1, h, 4), :] = high[h:]
    pairs[pl.ds(2, h, 4), :] = low[:h]
    pairs[pl.ds(3, h, 4), :] = low[h:]


def gram(pieces):
    _, rows, width = pieces.shape
    return pl.pallas_call(
        gram_kernel,
        out_shape=(
            jax.ShapeDtypeStruct((rows, width), F32),
            jax.ShapeDtypeStruct((2 * width, width), F32),
        ),
        in_specs=[VMEM],
        out_specs=(VMEM, VMEM),
        compiler_params=params(32),
        name="gram",
    )(pieces)


def add_kernel(given, summed):
    steps = given.shape[0] // 8
    total, error = given[0:8, :], jnp.zeros((8, given.shape[1]), F32)
    for k in range(1, steps):
        total, slip = two_sum(total, given[8 * k : 8 * k + 8, :])
        error = error + slip
    high, slip = two_sum(total[0:2], total[4:6])
    low = (error[0:2] + error[4:6]) + (total[2:4] + total[6:8]) + slip
    high, low = two_sum(high, low)
    chunk = jnp.concatenate([high, low, high, low], axis=0)
    for k in range(summed.shape[0] // 8):
        summed[8 * k : 8 * k + 8, :] = chunk


def add_pairs(given, copies):
    return pl.pallas_call(
        add_kernel,
        out_shape=jax.ShapeDtypeStruct((4 * copies, given.shape[1]), F32),
        in_specs=[VMEM],
        out_specs=VMEM,
        compiler_params=params(16),
        name="add_pairs",
    )(given)


PANEL = 8


def factor(rows):
    count = len(rows)
    width = PANEL * count
    place = lax.broadcasted_iota(jnp.int32, (PANEL, width), 0)
    lane = lax.broadcasted_iota(jnp.int32, (PANEL, width), 1)
    rows = list(rows)
    inverse = [(lane == place + PANEL * k).astype(F32) for k in range(count)]
    for k in range(count):
        a, x = rows[k], inverse[k]
        columns = [
            jnp.broadcast_to(a[:, PANEL * k + j : PANEL * k + j + 1], (PANEL, width)) for j in range(PANEL)
        ]
        scale = jnp.zeros((PANEL, width), F32)
        for j in range(PANEL):
            pivot = jnp.broadcast_to(columns[j][j : j + 1, :], (PANEL, width))
            root = lax.rsqrt(pivot)
            scale = jnp.where(place == j, root, scale)
            ratio = jnp.where(place > j, columns[j] * (root * root), 0.0)
            a = a - ratio * a[j : j + 1, :]
            x = x - ratio * x[j : j + 1, :]
            for l in range(j + 1, PANEL):
                columns[l] = columns[l] - ratio * columns[l][j : j + 1, :]
        a = jnp.where(lane >= place + PANEL * k, a * scale, 0.0)
        x = x * scale
        rows[k], inverse[k] = a, x
        if k + 1 < count:
            below = a[:, PANEL * (k + 1) :]
            change = mm(below, jnp.concatenate([a, x], axis=1), (0, 0))
            for i in range(k + 1, count):
                at = PANEL * (i - k - 1)
                rows[i] = rows[i] - change[at : at + PANEL, :width]
                inverse[i] = inverse[i] - change[at : at + PANEL, width:]
    return jnp.concatenate(rows, axis=0), jnp.concatenate(inverse, axis=0)


def panels(matrix):
    return [matrix[k : k + PANEL, :] for k in range(0, matrix.shape[0], PANEL)]


def finish_kernel(scale, pairs, sketch, basis, whole_r, one_r):
    width = sketch.shape[1]
    h = width // 2
    high = jnp.concatenate([pairs[pl.ds(0, h, 4), :], pairs[pl.ds(1, h, 4), :]], axis=0)
    low = jnp.concatenate([pairs[pl.ds(2, h, 4), :], pairs[pl.ds(3, h, 4), :]], axis=0)
    upper, inverse = factor(panels(high))
    parts = sliced(upper, 0, SLICES + 1)
    rest, carried = high, low
    for order in range(SLICES + 1):
        left = jnp.concatenate(parts[: order + 1], axis=0)
        right = jnp.concatenate(parts[: order + 1][::-1], axis=0)
        term = lax.dot_general(left, right, (((0,), (0,)), ((), ())), preferred_element_type=F32)
        rest, error = two_sum(rest, -term)
        carried = carried + error
    rest = rest + carried
    eye = lax.broadcasted_iota(jnp.int32, (width, width), 0) == lax.broadcasted_iota(
        jnp.int32, (width, width), 1
    )
    gram_two = mm(mm(inverse, rest), inverse, (1, 1)) + eye.astype(F32)
    upper_two, inverse_two = factor(panels(gram_two))
    both = mm(inverse_two, inverse)
    basis[...] = mm(sketch[...], both, (1, 1)) * scale[0]
    whole_r[...] = mm(upper_two, upper) / scale[0]
    one_r[...] = upper / scale[0]


def finish(pairs, sketch, scale):
    square = jax.ShapeDtypeStruct((sketch.shape[1],) * 2, F32)
    return pl.pallas_call(
        finish_kernel,
        out_shape=(jax.ShapeDtypeStruct(sketch.shape, F32), square, square),
        in_specs=[SMEM, VMEM, VMEM],
        out_specs=(VMEM, VMEM, VMEM),
        compiler_params=params(32),
        name="finish",
    )(scale.reshape(1), pairs, sketch)


def exchange(x, axes):
    return lax.all_to_all(x, axes, 0, 0, tiled=True)


def per_device(tile_values, tile_coords, tile_counts, omega):
    tile = tile_values.shape[2]
    width = omega.shape[1]
    keep, give = partial_sketch(tile_values, tile_coords, tile_counts, omega)
    got = lax.ppermute(give, "core", [(0, 1), (1, 0)])
    pieces = exchange(keep + got, "x")
    sketch, pairs = gram(pieces.reshape(4, HALF // 4 * tile, width))
    wide = ("y", "x", "core")
    pairs = add_pairs(exchange(pairs, wide), 8)
    pairs = add_pairs(exchange(pairs, "z"), 64)
    pairs = exchange(pairs, wide)
    total_rows = RB * tile * lax.axis_size(ROWS)
    return finish(pairs, sketch, jnp.sqrt(jnp.float32(total_rows)))


def solution(mesh):
    grid = Mesh(mesh.devices.reshape(8, 8, 4, 2), ("z", "y", "x", "core"))
    return jax.shard_map(
        per_device,
        mesh=grid,
        in_specs=(
            P(ROWS, COLUMNS, None),
            P(ROWS, COLUMNS),
            P(ROWS, COLUMNS),
            P(COLUMNS, None),
        ),
        out_specs=(P(ROWS + COLUMNS, None), P(), P()),
        check_vma=False,
    )
```

```python
import jax
import jax.numpy as jnp
from jax import lax
from jax.experimental import pallas as pl
from jax.experimental.pallas import tpu as pltpu
from jax.sharding import Mesh, PartitionSpec as P

RB = 32
HALF = RB // 2
PANEL = 8
GROUP = 8
ROWS = "z", "y"
COLUMNS = "x", "core"
F32 = jnp.float32
HIGHEST = lax.Precision.HIGHEST
VMEM = pl.BlockSpec(memory_space=pltpu.VMEM)
SMEM = pl.BlockSpec(memory_space=pltpu.SMEM)
HBM = pl.BlockSpec(memory_space=pltpu.HBM)


def params(mib):
    return pltpu.CompilerParams(vmem_limit_bytes=mib * 2**20)


def mm(a, b, contract=(1, 0)):
    return lax.dot_general(
        a,
        b,
        (((contract[0],), (contract[1],)), ((), ())),
        precision=HIGHEST,
        preferred_element_type=F32,
    )


def two_sum(a, b):
    total = a + b
    other = total - a
    return total, (a - (total - other)) + (b - other)


def sketch_kernel(coords, count, core, tiles, omega, total, held, blocks, products, fetched, ready):
    tile = held.shape[1]
    used = count[0, 0]
    groups = lax.div(used + (GROUP - 1), GROUP)
    mine = core[0]

    def fetch(g):
        part = pl.ds(pl.multiple_of(g * GROUP, GROUP), GROUP)
        return pltpu.make_async_copy(tiles.at[part], held.at[part], fetched.at[g])

    whole = pltpu.make_async_copy(omega, blocks, ready.at[0])
    whole.start()

    @pl.loop(0, groups)
    def _(g):
        fetch(g).start()

    total[...] = jnp.zeros_like(total)
    whole.wait()

    @pl.loop(0, groups)
    def _(g):
        fetch(g).wait()
        for u in range(GROUP):
            s = g * GROUP + u
            column = jnp.clip(coords[1, s], 0, blocks.shape[0] // tile - 1)
            block = blocks[pl.ds(pl.multiple_of(column * tile, tile), tile), :]
            products[u] = jnp.dot(held[s], block, preferred_element_type=F32)
        for u in range(GROUP):
            s = g * GROUP + u
            row = coords[0, s]
            x, rest = lax.div(row, 8), lax.rem(row, 8)
            own = (lax.div(rest, 4) == mine).astype(jnp.int32)
            place = own * HALF + x * 4 + lax.rem(rest, 4)
            place = jnp.where(s < used, jnp.clip(place, 0, RB - 1), RB)
            total[place] += products[u]


def partial_sketch(tile_values, tile_coords, tile_counts, omega):
    slots, tile, _ = tile_values.shape
    width = omega.shape[1]
    core = lax.axis_index("core").astype(jnp.int32).reshape(1)
    return pl.pallas_call(
        sketch_kernel,
        out_shape=jax.ShapeDtypeStruct((RB + 1, tile, width), F32),
        in_specs=[SMEM, SMEM, SMEM, HBM, HBM],
        out_specs=VMEM,
        scratch_shapes=[
            pltpu.VMEM((slots, tile, tile), jnp.bfloat16),
            pltpu.VMEM(omega.shape, jnp.bfloat16),
            pltpu.VMEM((GROUP, tile, width), F32),
            pltpu.SemaphoreType.DMA((slots // GROUP,)),
            pltpu.SemaphoreType.DMA((1,)),
        ],
        compiler_params=params(32),
        name="sketch",
    )(
        pltpu.with_memory_space_constraint(tile_coords.T, pltpu.HBM),
        tile_counts,
        core,
        pltpu.with_memory_space_constraint(tile_values, pltpu.HBM),
        pltpu.with_memory_space_constraint(omega, pltpu.HBM),
    )


SLICES = 4
BITS = 8


def sliced(x, axis, count):
    grid = jnp.max(jnp.abs(x), axis=axis, keepdims=True) * (2.0**17)
    parts = []
    for _ in range(count):
        part = ((x + grid) - grid).astype(jnp.bfloat16)
        x = x - part.astype(F32)
        grid = grid * (2.0**-BITS)
        parts.append(part)
    return parts


def pair_of(orders):
    high, low = orders[0], jnp.zeros_like(orders[0])
    for term in orders[1:]:
        high, error = two_sum(high, term)
        low = low + error
    return two_sum(high, low)


def gram_kernel(pieces, sketch, pairs):
    rows, width = sketch.shape
    x = (pieces[0] + pieces[1]) + (pieces[2] + pieces[3])
    sketch[...] = x
    parts = sliced(x, 0, SLICES)
    across = jnp.concatenate(parts, axis=1)
    orders = [None] * (SLICES + 2)
    for i in range(SLICES):
        reach = min(SLICES, SLICES + 1 - i)
        block = lax.dot_general(
            parts[i],
            across[:, : reach * width],
            (((0,), (0,)), ((), ())),
            preferred_element_type=F32,
        )
        for j in range(reach):
            term = block[:, j * width : (j + 1) * width]
            o = i + j
            orders[o] = term if orders[o] is None else orders[o] + term
    high, low = pair_of([o for o in orders if o is not None])
    for k in range(width // PANEL):
        at = slice(PANEL * k, PANEL * (k + 1))
        pairs[2 * PANEL * k : 2 * PANEL * k + PANEL, :] = high[at]
        pairs[2 * PANEL * k + PANEL : 2 * PANEL * (k + 1), :] = low[at]


def gram(pieces):
    _, rows, width = pieces.shape
    return pl.pallas_call(
        gram_kernel,
        out_shape=(
            jax.ShapeDtypeStruct((rows, width), F32),
            jax.ShapeDtypeStruct((2 * width, width), F32),
        ),
        in_specs=[VMEM],
        out_specs=(VMEM, VMEM),
        compiler_params=params(32),
        name="gram",
    )(pieces)


def add_kernel(given, summed):
    high, low = given[0:PANEL, :], given[PANEL : 2 * PANEL, :]
    for k in range(2 * PANEL, given.shape[0], 2 * PANEL):
        high, error = two_sum(high, given[k : k + PANEL, :])
        low = low + (given[k + PANEL : k + 2 * PANEL, :] + error)
    high, low = two_sum(high, low)
    for k in range(0, summed.shape[0], 2 * PANEL):
        summed[k : k + PANEL, :] = high
        summed[k + PANEL : k + 2 * PANEL, :] = low


def add_pairs(given, copies):
    return pl.pallas_call(
        add_kernel,
        out_shape=jax.ShapeDtypeStruct((2 * PANEL * copies, given.shape[1]), F32),
        in_specs=[VMEM],
        out_specs=VMEM,
        compiler_params=params(16),
        name="add_pairs",
    )(given)


def eliminate(a, x, k):
    shape = a.shape
    place = lax.broadcasted_iota(jnp.int32, shape, 0)
    columns = [jnp.broadcast_to(a[:, PANEL * k + j : PANEL * k + j + 1], shape) for j in range(PANEL)]
    scale = jnp.zeros(shape, F32)
    for j in range(PANEL):
        root = lax.rsqrt(jnp.broadcast_to(columns[j][j : j + 1, :], shape))
        scale = jnp.where(place == j, root, scale)
        ratio = jnp.where(place > j, columns[j] * (root * root), 0.0)
        a = a - ratio * a[j : j + 1, :]
        x = x - ratio * x[j : j + 1, :]
        for l in range(j + 1, PANEL):
            columns[l] = columns[l] - ratio * columns[l][j : j + 1, :]
    return a, x, scale


def factor(matrix):
    width = matrix.shape[0]
    count = width // PANEL
    place = lax.broadcasted_iota(jnp.int32, (PANEL, width), 0)
    lane = lax.broadcasted_iota(jnp.int32, (PANEL, width), 1)
    rows = [matrix[PANEL * k : PANEL * (k + 1), :] for k in range(count)]
    inverse = [(lane == place + PANEL * k).astype(F32) for k in range(count)]
    for k in range(count):
        near = slice(k, k + 2)
        a, x, scale = eliminate(jnp.concatenate(rows[near], axis=0), jnp.concatenate(inverse[near], axis=0), k)
        if k + 1 < count:
            rows[k + 1], inverse[k + 1] = a[PANEL:], x[PANEL:]
        a = jnp.where(lane >= place + PANEL * k, a[:PANEL] * scale[:PANEL], 0.0)
        x = x[:PANEL] * scale[:PANEL]
        rows[k], inverse[k] = a, x
        if k + 2 < count:
            change = mm(a[:, PANEL * (k + 2) :], jnp.concatenate([a, x], axis=1), (0, 0))
            for i in range(k + 2, count):
                at = PANEL * (i - k - 2)
                rows[i] = rows[i] - change[at : at + PANEL, :width]
                inverse[i] = inverse[i] - change[at : at + PANEL, width:]
    return jnp.concatenate(rows, axis=0), jnp.concatenate(inverse, axis=0)


def mm3(a, b, contract=(1, 0)):
    a_high, b_high = a.astype(jnp.bfloat16), b.astype(jnp.bfloat16)
    a_low = (a - a_high.astype(F32)).astype(jnp.bfloat16)
    b_low = (b - b_high.astype(F32)).astype(jnp.bfloat16)
    return lax.dot_general(
        jnp.concatenate([a_high, a_high, a_low], axis=contract[0]),
        jnp.concatenate([b_high, b_low, b_high], axis=contract[1]),
        (((contract[0],), (contract[1],)), ((), ())),
        preferred_element_type=F32,
    )


def finish_kernel(scale, pairs, sketch, basis, whole_r, one_r, upper_two, change_two):
    width = sketch.shape[1]
    chunks = range(0, 2 * width, 2 * PANEL)
    high = jnp.concatenate([pairs[k : k + PANEL, :] for k in chunks], axis=0)
    low = jnp.concatenate([pairs[k + PANEL : k + 2 * PANEL, :] for k in chunks], axis=0)
    place = lax.broadcasted_iota(jnp.int32, (width, width), 0)
    lane = lax.broadcasted_iota(jnp.int32, (width, width), 1)
    eye = (place == lane).astype(F32)
    upper, inverse = factor(high)
    one_r[...] = upper / scale[0]
    inverse = inverse - mm3(mm(inverse, upper, (1, 1)) - eye, inverse)
    parts = sliced(upper, 0, SLICES + 1)
    rest, carried = high, low
    for order in range(SLICES + 1):
        left = jnp.concatenate(parts[: order + 1], axis=0)
        right = jnp.concatenate(parts[: order + 1][::-1], axis=0)
        term = lax.dot_general(left, right, (((0,), (0,)), ((), ())), preferred_element_type=F32)
        rest, error = two_sum(rest, -term)
        carried = carried + error
    rest = rest + carried
    excess = mm3(mm3(inverse, rest), inverse, (1, 1))
    weight = jnp.where(place > lane, 1.0, jnp.where(place == lane, 0.5, 0.0))
    left, change = excess, None
    for _ in range(2):
        half = left * weight
        square = mm3(half, half)
        outer = mm3(half, half, (1, 1))
        third = mm3(half, outer)
        change = -half if change is None else change - half - mm3(half, change)
        left = (third + third.T) - (square + square.T + outer)
    change_two[...] = change
    lower_two = excess + change.T + mm3(excess, change, (1, 1))
    upper_two[...] = jnp.where(place <= lane, lower_two.T, 0.0) + eye

    @pl.when(jnp.logical_not(jnp.max(jnp.abs(left)) < 1e-6))
    def _():
        upper_full, inverse_full = factor(excess + eye)
        upper_two[...] = upper_full
        change_two[...] = inverse_full - eye

    both = inverse + mm3(change_two[...], inverse)
    basis[...] = mm(sketch[...], both, (1, 1)) * scale[0]
    whole_r[...] = (upper + mm3(upper_two[...] - eye, upper)) / scale[0]


def finish(pairs, sketch, scale):
    square = jax.ShapeDtypeStruct((sketch.shape[1],) * 2, F32)
    return pl.pallas_call(
        finish_kernel,
        out_shape=(jax.ShapeDtypeStruct(sketch.shape, F32), square, square),
        in_specs=[SMEM, VMEM, VMEM],
        out_specs=(VMEM, VMEM, VMEM),
        scratch_shapes=[pltpu.VMEM(square.shape, F32), pltpu.VMEM(square.shape, F32)],
        compiler_params=params(32),
        name="finish",
    )(scale.reshape(1), pairs, sketch)


def exchange(x, axes):
    return lax.all_to_all(x, axes, 0, 0, tiled=True)


def per_device(tile_values, tile_coords, tile_counts, omega):
    tile = tile_values.shape[2]
    width = omega.shape[1]
    partial = partial_sketch(tile_values, tile_coords, tile_counts, omega)
    got = lax.ppermute(partial[:HALF], "core", [(0, 1), (1, 0)])
    pieces = exchange(partial[HALF:RB] + got, "x")
    sketch, pairs = gram(pieces.reshape(4, HALF // 4 * tile, width))
    near, far = ("y", "core"), ("z", "x")
    pairs = add_pairs(exchange(pairs, near), 32)
    pairs = add_pairs(exchange(pairs, far), 16)
    pairs = exchange(pairs, near)
    total_rows = RB * tile * lax.axis_size(ROWS)
    return finish(pairs, sketch, jnp.sqrt(jnp.float32(total_rows)))


def solution(mesh):
    grid = Mesh(mesh.devices.reshape(8, 8, 4, 2), ("z", "y", "x", "core"))
    return jax.shard_map(
        per_device,
        mesh=grid,
        in_specs=(
            P(ROWS, COLUMNS, None),
            P(ROWS, COLUMNS),
            P(ROWS, COLUMNS),
            P(COLUMNS, None),
        ),
        out_specs=(P(ROWS + COLUMNS, None), P(), P()),
        check_vma=False,
    )
```

```python
import jax
import jax.numpy as jnp
from jax import lax
from jax.experimental import pallas as pl
from jax.experimental.pallas import tpu as pltpu
from jax.sharding import Mesh, PartitionSpec as P

RB = 32
HALF = RB // 2
PANEL = 8
AHEAD = 3
GROUP = 28
ROWS = "z", "y"
COLUMNS = "x", "core"
F32 = jnp.float32
HIGHEST = lax.Precision.HIGHEST
VMEM = pl.BlockSpec(memory_space=pltpu.VMEM)
SMEM = pl.BlockSpec(memory_space=pltpu.SMEM)
HBM = pl.BlockSpec(memory_space=pltpu.HBM)


def params(mib):
    return pltpu.CompilerParams(vmem_limit_bytes=mib * 2**20)


def mm(a, b, contract=(1, 0)):
    return lax.dot_general(
        a,
        b,
        (((contract[0],), (contract[1],)), ((), ())),
        precision=HIGHEST,
        preferred_element_type=F32,
    )


def two_sum(a, b):
    total = a + b
    other = total - a
    return total, (a - (total - other)) + (b - other)


def sketch_kernel(coords, count, core, tiles, omega, total, held, blocks, products, fetched, ready):
    tile = held.shape[1]
    used = count[0, 0]
    groups = lax.div(used + (GROUP - 1), GROUP)
    mine = core[0]

    def fetch(g):
        part = pl.ds(pl.multiple_of(g * GROUP, GROUP), GROUP)
        return pltpu.make_async_copy(tiles.at[part], held.at[part], fetched.at[g])

    whole = pltpu.make_async_copy(omega, blocks, ready.at[0])
    whole.start()

    @pl.loop(0, groups)
    def _(g):
        fetch(g).start()

    total[...] = jnp.zeros_like(total)
    whole.wait()

    @pl.loop(0, groups)
    def _(g):
        fetch(g).wait()
        for u in range(GROUP):
            s = g * GROUP + u
            column = jnp.clip(coords[1, s], 0, blocks.shape[0] // tile - 1)
            block = blocks[pl.ds(pl.multiple_of(column * tile, tile), tile), :]
            products[u] = jnp.dot(held[s], block, preferred_element_type=F32)
        for u in range(GROUP):
            s = g * GROUP + u
            row = coords[0, s]
            x, rest = lax.div(row, 8), lax.rem(row, 8)
            own = (lax.div(rest, 4) == mine).astype(jnp.int32)
            place = own * HALF + x * 4 + lax.rem(rest, 4)
            place = jnp.where(s < used, jnp.clip(place, 0, RB - 1), RB)
            total[place] += products[u]


def partial_sketch(tile_values, tile_coords, tile_counts, omega):
    slots, tile, _ = tile_values.shape
    width = omega.shape[1]
    core = lax.axis_index("core").astype(jnp.int32).reshape(1)
    return pl.pallas_call(
        sketch_kernel,
        out_shape=jax.ShapeDtypeStruct((RB + 1, tile, width), F32),
        in_specs=[SMEM, SMEM, SMEM, HBM, HBM],
        out_specs=VMEM,
        scratch_shapes=[
            pltpu.VMEM((slots, tile, tile), jnp.bfloat16),
            pltpu.VMEM(omega.shape, jnp.bfloat16),
            pltpu.VMEM((GROUP, tile, width), F32),
            pltpu.SemaphoreType.DMA((slots // GROUP,)),
            pltpu.SemaphoreType.DMA((1,)),
        ],
        compiler_params=params(32),
        name="sketch",
    )(
        pltpu.with_memory_space_constraint(tile_coords.T, pltpu.HBM),
        tile_counts,
        core,
        pltpu.with_memory_space_constraint(tile_values, pltpu.HBM),
        pltpu.with_memory_space_constraint(omega, pltpu.HBM),
    )


SLICES = 4
BITS = 8


def sliced(x, axis, count):
    grid = jnp.max(jnp.abs(x), axis=axis, keepdims=True) * (2.0**17)
    parts = []
    for _ in range(count):
        part = ((x + grid) - grid).astype(jnp.bfloat16)
        x = x - part.astype(F32)
        grid = grid * (2.0**-BITS)
        parts.append(part)
    return parts


def pair_of(orders):
    high, low = orders[0], jnp.zeros_like(orders[0])
    for term in orders[1:]:
        high, error = two_sum(high, term)
        low = low + error
    return two_sum(high, low)


def gram_kernel(pieces, sketch, pairs):
    rows, width = sketch.shape
    x = (pieces[0] + pieces[1]) + (pieces[2] + pieces[3])
    sketch[...] = x
    parts = sliced(x, 0, SLICES)
    across = jnp.concatenate(parts, axis=1)
    orders = [None] * (SLICES + 2)
    for i in range(SLICES):
        reach = min(SLICES, SLICES + 1 - i)
        block = lax.dot_general(
            parts[i],
            across[:, : reach * width],
            (((0,), (0,)), ((), ())),
            preferred_element_type=F32,
        )
        for j in range(reach):
            term = block[:, j * width : (j + 1) * width]
            o = i + j
            orders[o] = term if orders[o] is None else orders[o] + term
    high, low = pair_of([o for o in orders if o is not None])
    for k in range(width // PANEL):
        at = slice(PANEL * k, PANEL * (k + 1))
        pairs[2 * PANEL * k : 2 * PANEL * k + PANEL, :] = high[at]
        pairs[2 * PANEL * k + PANEL : 2 * PANEL * (k + 1), :] = low[at]


def gram(pieces):
    _, rows, width = pieces.shape
    return pl.pallas_call(
        gram_kernel,
        out_shape=(
            jax.ShapeDtypeStruct((rows, width), F32),
            jax.ShapeDtypeStruct((2 * width, width), F32),
        ),
        in_specs=[VMEM],
        out_specs=(VMEM, VMEM),
        compiler_params=params(32),
        name="gram",
    )(pieces)


def add_kernel(given, summed):
    high, low = given[0:PANEL, :], given[PANEL : 2 * PANEL, :]
    for k in range(2 * PANEL, given.shape[0], 2 * PANEL):
        high, error = two_sum(high, given[k : k + PANEL, :])
        low = low + (given[k + PANEL : k + 2 * PANEL, :] + error)
    high, low = two_sum(high, low)
    for k in range(0, summed.shape[0], 2 * PANEL):
        summed[k : k + PANEL, :] = high
        summed[k + PANEL : k + 2 * PANEL, :] = low


def add_pairs(given, copies):
    return pl.pallas_call(
        add_kernel,
        out_shape=jax.ShapeDtypeStruct((2 * PANEL * copies, given.shape[1]), F32),
        in_specs=[VMEM],
        out_specs=VMEM,
        compiler_params=params(16),
        name="add_pairs",
    )(given)


def eliminate(a, x, k):
    shape = a.shape
    place = lax.broadcasted_iota(jnp.int32, shape, 0)
    columns = [jnp.broadcast_to(a[:, PANEL * k + j : PANEL * k + j + 1], shape) for j in range(PANEL)]
    scale = jnp.zeros(shape, F32)
    for j in range(PANEL):
        root = lax.rsqrt(jnp.broadcast_to(columns[j][j : j + 1, :], shape))
        scale = jnp.where(place == j, root, scale)
        ratio = jnp.where(place > j, columns[j] * (root * root), 0.0)
        a = a - ratio * a[j : j + 1, :]
        x = x - ratio * x[j : j + 1, :]
        for l in range(j + 1, PANEL):
            columns[l] = columns[l] - ratio * columns[l][j : j + 1, :]
    return a, x, scale


def factor(matrix):
    width = matrix.shape[0]
    count = width // PANEL
    place = lax.broadcasted_iota(jnp.int32, (PANEL, width), 0)
    lane = lax.broadcasted_iota(jnp.int32, (PANEL, width), 1)
    rows = [matrix[PANEL * k : PANEL * (k + 1), :] for k in range(count)]
    inverse = [(lane == place + PANEL * k).astype(F32) for k in range(count)]
    for k in range(count):
        near = range(k, min(k + AHEAD, count))
        a, x, scale = eliminate(
            jnp.concatenate([rows[i] for i in near], axis=0),
            jnp.concatenate([inverse[i] for i in near], axis=0),
            k,
        )
        for i in near:
            at = slice(PANEL * (i - k), PANEL * (i - k + 1))
            rows[i], inverse[i] = a[at], x[at]
        rows[k] = jnp.where(lane >= place + PANEL * k, rows[k] * scale[:PANEL], 0.0)
        inverse[k] = inverse[k] * scale[:PANEL]
        if k + AHEAD < count:
            change = outer(rows[k], jnp.concatenate([rows[k], inverse[k]], axis=1))
            for i in range(k + AHEAD, count):
                at = slice(PANEL * i, PANEL * (i + 1))
                rows[i] = rows[i] - change[at, :width]
                inverse[i] = inverse[i] - change[at, width:]
    return jnp.concatenate(rows, axis=0), jnp.concatenate(inverse, axis=0)


def thirds(x):
    high = x.astype(jnp.bfloat16).astype(F32)
    rest = x - high
    middle = rest.astype(jnp.bfloat16).astype(F32)
    return high, middle, rest - middle


def outer(a, b):
    ah, am, al = thirds(a)
    bh, bm, bl = thirds(b)
    return lax.dot_general(
        jnp.concatenate([ah, ah, am, ah, am, al], axis=0).astype(jnp.bfloat16),
        jnp.concatenate([bh, bm, bh, bl, bm, bh], axis=0).astype(jnp.bfloat16),
        (((0,), (0,)), ((), ())),
        preferred_element_type=F32,
    )


def mm3(a, b, contract=(1, 0)):
    a_high, b_high = a.astype(jnp.bfloat16), b.astype(jnp.bfloat16)
    a_low = (a - a_high.astype(F32)).astype(jnp.bfloat16)
    b_low = (b - b_high.astype(F32)).astype(jnp.bfloat16)
    return lax.dot_general(
        jnp.concatenate([a_high, a_high, a_low], axis=contract[0]),
        jnp.concatenate([b_high, b_low, b_high], axis=contract[1]),
        (((contract[0],), (contract[1],)), ((), ())),
        preferred_element_type=F32,
    )


def finish_kernel(scale, pairs, sketch, basis, whole_r, one_r, upper_two, change_two):
    width = sketch.shape[1]
    chunks = range(0, 2 * width, 2 * PANEL)
    high = jnp.concatenate([pairs[k : k + PANEL, :] for k in chunks], axis=0)
    low = jnp.concatenate([pairs[k + PANEL : k + 2 * PANEL, :] for k in chunks], axis=0)
    place = lax.broadcasted_iota(jnp.int32, (width, width), 0)
    lane = lax.broadcasted_iota(jnp.int32, (width, width), 1)
    eye = (place == lane).astype(F32)
    upper, inverse = factor(high)
    one_r[...] = upper / scale[0]
    inverse = inverse - mm3(mm(inverse, upper, (1, 1)) - eye, inverse)
    parts = sliced(upper, 0, SLICES + 1)
    rest, carried = high, low
    for order in range(SLICES + 1):
        left = jnp.concatenate(parts[: order + 1], axis=0)
        right = jnp.concatenate(parts[: order + 1][::-1], axis=0)
        term = lax.dot_general(left, right, (((0,), (0,)), ((), ())), preferred_element_type=F32)
        rest, error = two_sum(rest, -term)
        carried = carried + error
    rest = rest + carried
    excess = mm3(mm3(inverse, rest), inverse, (1, 1))
    weight = jnp.where(place > lane, 1.0, jnp.where(place == lane, 0.5, 0.0))
    left, change = excess, None
    for _ in range(2):
        half = left * weight
        square = mm3(half, half)
        sides = mm3(half, half, (1, 1))
        third = mm3(half, sides)
        change = -half if change is None else change - half - mm3(half, change)
        left = (third + third.T) - (square + square.T + sides)
    change_two[...] = change
    lower_two = excess + change.T + mm3(excess, change, (1, 1))
    upper_two[...] = jnp.where(place <= lane, lower_two.T, 0.0) + eye

    @pl.when(jnp.logical_not(jnp.max(jnp.abs(left)) < 1e-6))
    def _():
        upper_full, inverse_full = factor(excess + eye)
        upper_two[...] = upper_full
        change_two[...] = inverse_full - eye

    both = inverse + mm3(change_two[...], inverse)
    basis[...] = mm(sketch[...], both, (1, 1)) * scale[0]
    whole_r[...] = (upper + mm3(upper_two[...] - eye, upper)) / scale[0]


def finish(pairs, sketch, scale):
    square = jax.ShapeDtypeStruct((sketch.shape[1],) * 2, F32)
    return pl.pallas_call(
        finish_kernel,
        out_shape=(jax.ShapeDtypeStruct(sketch.shape, F32), square, square),
        in_specs=[SMEM, VMEM, VMEM],
        out_specs=(VMEM, VMEM, VMEM),
        scratch_shapes=[pltpu.VMEM(square.shape, F32), pltpu.VMEM(square.shape, F32)],
        compiler_params=params(32),
        name="finish",
    )(scale.reshape(1), pairs, sketch)


def exchange(x, axes):
    return lax.all_to_all(x, axes, 0, 0, tiled=True)


def per_device(tile_values, tile_coords, tile_counts, omega):
    tile = tile_values.shape[2]
    width = omega.shape[1]
    partial = partial_sketch(tile_values, tile_coords, tile_counts, omega)
    got = lax.ppermute(partial[:HALF], "core", [(0, 1), (1, 0)])
    pieces = exchange(partial[HALF:RB] + got, "x")
    sketch, pairs = gram(pieces.reshape(4, HALF // 4 * tile, width))
    near, far = ("y", "core"), ("z", "x")
    pairs = add_pairs(exchange(pairs, near), 32)
    pairs = add_pairs(exchange(pairs, far), 16)
    pairs = exchange(pairs, near)
    total_rows = RB * tile * lax.axis_size(ROWS)
    return finish(pairs, sketch, jnp.sqrt(jnp.float32(total_rows)))


def solution(mesh):
    grid = Mesh(mesh.devices.reshape(8, 8, 4, 2), ("z", "y", "x", "core"))
    return jax.shard_map(
        per_device,
        mesh=grid,
        in_specs=(
            P(ROWS, COLUMNS, None),
            P(ROWS, COLUMNS),
            P(ROWS, COLUMNS),
            P(COLUMNS, None),
        ),
        out_specs=(P(ROWS + COLUMNS, None), P(), P()),
        check_vma=False,
    )
```

```python
import jax
import jax.numpy as jnp
from jax import lax
from jax.experimental import pallas as pl
from jax.experimental.pallas import tpu as pltpu
from jax.sharding import Mesh, PartitionSpec as P

RB = 32
HALF = RB // 2
PANEL = 8
AHEAD = 3
GROUP = 28
ROWS = "z", "y"
COLUMNS = "x", "core"
F32 = jnp.float32
HIGHEST = lax.Precision.HIGHEST
VMEM = pl.BlockSpec(memory_space=pltpu.VMEM)
SMEM = pl.BlockSpec(memory_space=pltpu.SMEM)
HBM = pl.BlockSpec(memory_space=pltpu.HBM)


def params(mib):
    return pltpu.CompilerParams(vmem_limit_bytes=mib * 2**20)


def mm(a, b, contract=(1, 0)):
    return lax.dot_general(
        a,
        b,
        (((contract[0],), (contract[1],)), ((), ())),
        precision=HIGHEST,
        preferred_element_type=F32,
    )


def two_sum(a, b):
    total = a + b
    other = total - a
    return total, (a - (total - other)) + (b - other)


def sketch_kernel(coords, count, core, tiles, omega, total, held, blocks, products, fetched, ready):
    tile = held.shape[1]
    used = count[0, 0]
    groups = lax.div(used + (GROUP - 1), GROUP)
    mine = core[0]

    def fetch(g):
        part = pl.ds(pl.multiple_of(g * GROUP, GROUP), GROUP)
        return pltpu.make_async_copy(tiles.at[part], held.at[part], fetched.at[g])

    whole = pltpu.make_async_copy(omega, blocks, ready.at[0])
    whole.start()

    @pl.loop(0, groups)
    def _(g):
        fetch(g).start()

    total[...] = jnp.zeros_like(total)
    whole.wait()

    @pl.loop(0, groups)
    def _(g):
        fetch(g).wait()
        for u in range(GROUP):
            s = g * GROUP + u
            column = jnp.clip(coords[1, s], 0, blocks.shape[0] // tile - 1)
            block = blocks[pl.ds(pl.multiple_of(column * tile, tile), tile), :]
            products[u] = jnp.dot(held[s], block, preferred_element_type=F32)
        for u in range(GROUP):
            s = g * GROUP + u
            row = coords[0, s]
            x, rest = lax.div(row, 8), lax.rem(row, 8)
            own = (lax.div(rest, 4) == mine).astype(jnp.int32)
            place = own * HALF + x * 4 + lax.rem(rest, 4)
            place = jnp.where(s < used, jnp.clip(place, 0, RB - 1), RB)
            total[place] += products[u]


def partial_sketch(tile_values, tile_coords, tile_counts, omega):
    slots, tile, _ = tile_values.shape
    width = omega.shape[1]
    core = lax.axis_index("core").astype(jnp.int32).reshape(1)
    return pl.pallas_call(
        sketch_kernel,
        out_shape=jax.ShapeDtypeStruct((RB + 1, tile, width), F32),
        in_specs=[SMEM, SMEM, SMEM, HBM, HBM],
        out_specs=VMEM,
        scratch_shapes=[
            pltpu.VMEM((slots, tile, tile), jnp.bfloat16),
            pltpu.VMEM(omega.shape, jnp.bfloat16),
            pltpu.VMEM((GROUP, tile, width), F32),
            pltpu.SemaphoreType.DMA((slots // GROUP,)),
            pltpu.SemaphoreType.DMA((1,)),
        ],
        compiler_params=params(32),
        name="sketch",
    )(
        pltpu.with_memory_space_constraint(tile_coords.T, pltpu.HBM),
        tile_counts,
        core,
        pltpu.with_memory_space_constraint(tile_values, pltpu.HBM),
        pltpu.with_memory_space_constraint(omega, pltpu.HBM),
    )


SLICES = 4
BITS = 8


def sliced(x, axis, count):
    grid = jnp.max(jnp.abs(x), axis=axis, keepdims=True) * (2.0**17)
    parts = []
    for _ in range(count):
        part = ((x + grid) - grid).astype(jnp.bfloat16)
        x = x - part.astype(F32)
        grid = grid * (2.0**-BITS)
        parts.append(part)
    return parts


def pair_of(orders):
    high, low = orders[0], jnp.zeros_like(orders[0])
    for term in orders[1:]:
        high, error = two_sum(high, term)
        low = low + error
    return two_sum(high, low)


def gram_kernel(pieces, sketch, pairs):
    rows, width = sketch.shape
    x = (pieces[0] + pieces[1]) + (pieces[2] + pieces[3])
    sketch[...] = x
    parts = sliced(x, 0, SLICES)
    across = jnp.concatenate(parts, axis=1)
    orders = [None] * (SLICES + 2)
    for i in range(SLICES):
        reach = min(SLICES, SLICES + 1 - i)
        block = lax.dot_general(
            parts[i],
            across[:, : reach * width],
            (((0,), (0,)), ((), ())),
            preferred_element_type=F32,
        )
        for j in range(reach):
            term = block[:, j * width : (j + 1) * width]
            o = i + j
            orders[o] = term if orders[o] is None else orders[o] + term
    high, low = pair_of([o for o in orders if o is not None])
    for k in range(width // PANEL):
        at = slice(PANEL * k, PANEL * (k + 1))
        pairs[2 * PANEL * k : 2 * PANEL * k + PANEL, :] = high[at]
        pairs[2 * PANEL * k + PANEL : 2 * PANEL * (k + 1), :] = low[at]


def gram(pieces):
    _, rows, width = pieces.shape
    return pl.pallas_call(
        gram_kernel,
        out_shape=(
            jax.ShapeDtypeStruct((rows, width), F32),
            jax.ShapeDtypeStruct((2 * width, width), F32),
        ),
        in_specs=[VMEM],
        out_specs=(VMEM, VMEM),
        compiler_params=params(32),
        name="gram",
    )(pieces)


def add_kernel(given, summed):
    high, low = given[0:PANEL, :], given[PANEL : 2 * PANEL, :]
    for k in range(2 * PANEL, given.shape[0], 2 * PANEL):
        high, error = two_sum(high, given[k : k + PANEL, :])
        low = low + (given[k + PANEL : k + 2 * PANEL, :] + error)
    high, low = two_sum(high, low)
    for k in range(0, summed.shape[0], 2 * PANEL):
        summed[k : k + PANEL, :] = high
        summed[k + PANEL : k + 2 * PANEL, :] = low


def add_pairs(given, copies):
    return pl.pallas_call(
        add_kernel,
        out_shape=jax.ShapeDtypeStruct((2 * PANEL * copies, given.shape[1]), F32),
        in_specs=[VMEM],
        out_specs=VMEM,
        compiler_params=params(16),
        name="add_pairs",
    )(given)


def spread(rows, at):
    return [jnp.broadcast_to(rows[:, at + j : at + j + 1], rows.shape) for j in range(PANEL)]


def factor(matrix):
    width = matrix.shape[0]
    count = width // PANEL
    shape = (PANEL, width)
    place = lax.broadcasted_iota(jnp.int32, shape, 0)
    lane = lax.broadcasted_iota(jnp.int32, shape, 1)
    rows = [matrix[PANEL * k : PANEL * (k + 1), :] for k in range(count)]
    inverse = [(lane == place + PANEL * k).astype(F32) for k in range(count)]
    columns = {}
    for k in range(count):
        near = range(k, min(k + AHEAD, count))
        for i in near:
            if i not in columns:
                columns[i] = spread(rows[i], PANEL * k)
        later = {i: spread(rows[i], PANEL * (k + 1)) if k + 1 < count else [] for i in near}
        scale = jnp.zeros(shape, F32)
        for j in range(PANEL):
            root = lax.rsqrt(jnp.broadcast_to(columns[k][j][j : j + 1, :], shape))
            scale = jnp.where(place == j, root, scale)
            ratio = {i: columns[i][j] * (root * root) for i in near}
            ratio[k] = jnp.where(place > j, ratio[k], 0.0)
            row, unit = rows[k][j : j + 1, :], inverse[k][j : j + 1, :]
            now = [c[j : j + 1, :] for c in columns[k]]
            next_ = [c[j : j + 1, :] for c in later[k]]
            for i in near:
                rows[i] = rows[i] - ratio[i] * row
                inverse[i] = inverse[i] - ratio[i] * unit
                for l in range(j + 1, PANEL):
                    columns[i][l] = columns[i][l] - ratio[i] * now[l]
                later[i] = [c - ratio[i] * d for c, d in zip(later[i], next_)]
        rows[k] = jnp.where(lane >= place + PANEL * k, rows[k] * scale, 0.0)
        inverse[k] = inverse[k] * scale
        columns = {i: later[i] for i in near if i > k}
        if k + AHEAD < count:
            change = outer(rows[k], jnp.concatenate([rows[k], inverse[k]], axis=1))
            for i in range(k + AHEAD, count):
                at = slice(PANEL * i, PANEL * (i + 1))
                rows[i] = rows[i] - change[at, :width]
                inverse[i] = inverse[i] - change[at, width:]
    return jnp.concatenate(rows, axis=0), jnp.concatenate(inverse, axis=0)


def thirds(x):
    high = x.astype(jnp.bfloat16).astype(F32)
    rest = x - high
    middle = rest.astype(jnp.bfloat16).astype(F32)
    return high, middle, rest - middle


def outer(a, b):
    ah, am, al = thirds(a)
    bh, bm, bl = thirds(b)
    return lax.dot_general(
        jnp.concatenate([ah, ah, am, ah, am, al], axis=0).astype(jnp.bfloat16),
        jnp.concatenate([bh, bm, bh, bl, bm, bh], axis=0).astype(jnp.bfloat16),
        (((0,), (0,)), ((), ())),
        preferred_element_type=F32,
    )


def mm3(a, b, contract=(1, 0)):
    a_high, b_high = a.astype(jnp.bfloat16), b.astype(jnp.bfloat16)
    a_low = (a - a_high.astype(F32)).astype(jnp.bfloat16)
    b_low = (b - b_high.astype(F32)).astype(jnp.bfloat16)
    return lax.dot_general(
        jnp.concatenate([a_high, a_high, a_low], axis=contract[0]),
        jnp.concatenate([b_high, b_low, b_high], axis=contract[1]),
        (((contract[0],), (contract[1],)), ((), ())),
        preferred_element_type=F32,
    )


def finish_kernel(scale, pairs, sketch, basis, whole_r, one_r, upper_two, change_two):
    width = sketch.shape[1]
    chunks = range(0, 2 * width, 2 * PANEL)
    high = jnp.concatenate([pairs[k : k + PANEL, :] for k in chunks], axis=0)
    low = jnp.concatenate([pairs[k + PANEL : k + 2 * PANEL, :] for k in chunks], axis=0)
    place = lax.broadcasted_iota(jnp.int32, (width, width), 0)
    lane = lax.broadcasted_iota(jnp.int32, (width, width), 1)
    eye = (place == lane).astype(F32)
    upper, inverse = factor(high)
    one_r[...] = upper / scale[0]
    basis_one = mm(sketch[...], inverse, (1, 1))
    flaw = mm(inverse, upper, (1, 1)) - eye
    parts = sliced(upper, 0, SLICES + 1)
    rest, carried = high, low
    for order in range(SLICES + 1):
        left = jnp.concatenate(parts[: order + 1], axis=0)
        right = jnp.concatenate(parts[: order + 1][::-1], axis=0)
        term = lax.dot_general(left, right, (((0,), (0,)), ((), ())), preferred_element_type=F32)
        rest, error = two_sum(rest, -term)
        carried = carried + error
    rest = rest + carried
    excess = mm3(mm3(inverse, rest), inverse, (1, 1)) + (flaw + flaw.T + mm3(flaw, flaw, (1, 1)))
    weight = jnp.where(place > lane, 1.0, jnp.where(place == lane, 0.5, 0.0))
    half = excess * weight
    square = mm3(half, half)
    sides = mm3(half, half, (1, 1))
    third = mm3(half, sides)
    left = (third + third.T) - (square + square.T + sides)
    last = left * weight
    change = mm3(last, half) - (half + last)
    change_two[...] = change
    lower_two = excess + change.T + mm3(excess, change, (1, 1))
    upper_two[...] = jnp.where(place <= lane, lower_two.T, 0.0)

    @pl.when(jnp.logical_not(jnp.sum(last * last) < 3e-7))
    def _():
        upper_full, inverse_full = factor(excess + eye)
        upper_two[...] = upper_full - eye
        change_two[...] = inverse_full - eye

    basis[...] = (basis_one + mm3(basis_one, change_two[...], (1, 1))) * scale[0]
    upper = upper - mm3(flaw, upper - mm3(flaw, upper, (0, 0)), (0, 0))
    whole_r[...] = (upper + mm3(upper_two[...], upper)) / scale[0]


def finish(pairs, sketch, scale):
    square = jax.ShapeDtypeStruct((sketch.shape[1],) * 2, F32)
    return pl.pallas_call(
        finish_kernel,
        out_shape=(jax.ShapeDtypeStruct(sketch.shape, F32), square, square),
        in_specs=[SMEM, VMEM, VMEM],
        out_specs=(VMEM, VMEM, VMEM),
        scratch_shapes=[pltpu.VMEM(square.shape, F32), pltpu.VMEM(square.shape, F32)],
        compiler_params=params(32),
        name="finish",
    )(scale.reshape(1), pairs, sketch)


def exchange(x, axes):
    return lax.all_to_all(x, axes, 0, 0, tiled=True)


def per_device(tile_values, tile_coords, tile_counts, omega):
    tile = tile_values.shape[2]
    width = omega.shape[1]
    partial = partial_sketch(tile_values, tile_coords, tile_counts, omega)
    got = lax.ppermute(partial[:HALF], "core", [(0, 1), (1, 0)])
    pieces = exchange(partial[HALF:RB] + got, "x")
    sketch, pairs = gram(pieces.reshape(4, HALF // 4 * tile, width))
    near, far = ("y", "core"), ("z", "x")
    pairs = add_pairs(exchange(pairs, near), 32)
    pairs = add_pairs(exchange(pairs, far), 16)
    pairs = exchange(pairs, near)
    total_rows = RB * tile * lax.axis_size(ROWS)
    return finish(pairs, sketch, jnp.sqrt(jnp.float32(total_rows)))


def solution(mesh):
    grid = Mesh(mesh.devices.reshape(8, 8, 4, 2), ("z", "y", "x", "core"))
    return jax.shard_map(
        per_device,
        mesh=grid,
        in_specs=(
            P(ROWS, COLUMNS, None),
            P(ROWS, COLUMNS),
            P(ROWS, COLUMNS),
            P(COLUMNS, None),
        ),
        out_specs=(P(ROWS + COLUMNS, None), P(), P()),
        check_vma=False,
    )
```

```python
import jax
import jax.numpy as jnp
from jax import lax
from jax.experimental import pallas as pl
from jax.experimental.pallas import tpu as pltpu
from jax.sharding import Mesh, PartitionSpec as P

RB = 32
HALF = RB // 2
CHUNK = 4
PANEL = 8
AHEAD = 3
GROUP = 28
ROWS = "z", "y"
COLUMNS = "x", "core"
F32 = jnp.float32
HIGHEST = lax.Precision.HIGHEST
VMEM = pl.BlockSpec(memory_space=pltpu.VMEM)
SMEM = pl.BlockSpec(memory_space=pltpu.SMEM)
HBM = pl.BlockSpec(memory_space=pltpu.HBM)


def params(mib):
    return pltpu.CompilerParams(vmem_limit_bytes=mib * 2**20)


def mm(a, b, contract=(1, 0)):
    return lax.dot_general(
        a,
        b,
        (((contract[0],), (contract[1],)), ((), ())),
        precision=HIGHEST,
        preferred_element_type=F32,
    )


def two_sum(a, b):
    total = a + b
    other = total - a
    return total, (a - (total - other)) + (b - other)


def sketch_kernel(coords, count, core, tiles, omega, total, held, blocks, products, fetched, ready):
    tile = held.shape[1]
    used = count[0, 0]
    groups = lax.div(used + (GROUP - 1), GROUP)
    mine = core[0]

    def fetch(g):
        part = pl.ds(pl.multiple_of(g * GROUP, GROUP), GROUP)
        return pltpu.make_async_copy(tiles.at[part], held.at[part], fetched.at[g])

    whole = pltpu.make_async_copy(omega, blocks, ready.at[0])
    whole.start()

    @pl.loop(0, groups)
    def _(g):
        fetch(g).start()

    total[...] = jnp.zeros_like(total)
    whole.wait()

    @pl.loop(0, groups)
    def _(g):
        fetch(g).wait()
        for u in range(GROUP):
            s = g * GROUP + u
            column = jnp.clip(coords[1, s], 0, blocks.shape[0] // tile - 1)
            block = blocks[pl.ds(pl.multiple_of(column * tile, tile), tile), :]
            products[u] = jnp.dot(held[s], block, preferred_element_type=F32)
        for u in range(GROUP):
            s = g * GROUP + u
            row = coords[0, s]
            x, rest = lax.div(row, 8), lax.rem(row, 8)
            own = (lax.div(rest, 4) == mine).astype(jnp.int32)
            place = own * HALF + x * 4 + lax.rem(rest, 4)
            place = jnp.where(s < used, jnp.clip(place, 0, RB - 1), RB)
            total[place] += products[u]


def partial_sketch(tile_values, tile_coords, tile_counts, omega):
    slots, tile, _ = tile_values.shape
    width = omega.shape[1]
    core = lax.axis_index("core").astype(jnp.int32).reshape(1)
    return pl.pallas_call(
        sketch_kernel,
        out_shape=jax.ShapeDtypeStruct((RB + 1, tile, width), F32),
        in_specs=[SMEM, SMEM, SMEM, HBM, HBM],
        out_specs=VMEM,
        scratch_shapes=[
            pltpu.VMEM((slots, tile, tile), jnp.bfloat16),
            pltpu.VMEM(omega.shape, jnp.bfloat16),
            pltpu.VMEM((GROUP, tile, width), F32),
            pltpu.SemaphoreType.DMA((slots // GROUP,)),
            pltpu.SemaphoreType.DMA((1,)),
        ],
        compiler_params=params(32),
        name="sketch",
    )(
        pltpu.with_memory_space_constraint(tile_coords.T, pltpu.HBM),
        tile_counts,
        core,
        pltpu.with_memory_space_constraint(tile_values, pltpu.HBM),
        pltpu.with_memory_space_constraint(omega, pltpu.HBM),
    )


SLICES = 4
BITS = 8


def sliced(x, axis, count):
    grid = jnp.max(jnp.abs(x), axis=axis, keepdims=True) * (2.0**17)
    parts = []
    for _ in range(count):
        part = ((x + grid) - grid).astype(jnp.bfloat16)
        x = x - part.astype(F32)
        grid = grid * (2.0**-BITS)
        parts.append(part)
    return parts


def pair_of(orders):
    high, low = orders[0], jnp.zeros_like(orders[0])
    for term in orders[1:]:
        high, error = two_sum(high, term)
        low = low + error
    return two_sum(high, low)


def gram_kernel(pieces, sketch, pairs):
    rows, width = sketch.shape
    x = (pieces[0] + pieces[1]) + (pieces[2] + pieces[3])
    sketch[...] = x
    parts = sliced(x, 0, SLICES)
    across = jnp.concatenate(parts, axis=1)
    orders = [None] * (SLICES + 2)
    for i in range(SLICES):
        reach = min(SLICES, SLICES + 1 - i)
        block = lax.dot_general(
            parts[i],
            across[:, : reach * width],
            (((0,), (0,)), ((), ())),
            preferred_element_type=F32,
        )
        for j in range(reach):
            term = block[:, j * width : (j + 1) * width]
            o = i + j
            orders[o] = term if orders[o] is None else orders[o] + term
    high, low = pair_of([o for o in orders if o is not None])
    for k in range(width // CHUNK):
        at = slice(CHUNK * k, CHUNK * (k + 1))
        pairs[2 * CHUNK * k : 2 * CHUNK * (k + 1), :] = jnp.concatenate([high[at], low[at]], axis=0)


def gram(pieces):
    _, rows, width = pieces.shape
    return pl.pallas_call(
        gram_kernel,
        out_shape=(
            jax.ShapeDtypeStruct((rows, width), F32),
            jax.ShapeDtypeStruct((2 * width, width), F32),
        ),
        in_specs=[VMEM],
        out_specs=(VMEM, VMEM),
        compiler_params=params(32),
        name="gram",
    )(pieces)


def add_kernel(given, summed):
    step = 2 * CHUNK
    total, error = given[0:step, :], jnp.zeros((step, given.shape[1]), F32)
    for k in range(step, given.shape[0], step):
        total, slip = two_sum(total, given[k : k + step, :])
        error = error + slip
    high, low = two_sum(total[:CHUNK], total[CHUNK:] + error[:CHUNK])
    chunk = jnp.concatenate([high, low], axis=0)
    for k in range(0, summed.shape[0], step):
        summed[k : k + step, :] = chunk


def add_pairs(given, copies):
    return pl.pallas_call(
        add_kernel,
        out_shape=jax.ShapeDtypeStruct((2 * CHUNK * copies, given.shape[1]), F32),
        in_specs=[VMEM],
        out_specs=VMEM,
        compiler_params=params(16),
        name="add_pairs",
    )(given)


def spread(rows, at):
    return [jnp.broadcast_to(rows[:, at + j : at + j + 1], rows.shape) for j in range(PANEL)]


def factor(matrix):
    width = matrix.shape[0]
    count = width // PANEL
    shape = (PANEL, width)
    place = lax.broadcasted_iota(jnp.int32, shape, 0)
    lane = lax.broadcasted_iota(jnp.int32, shape, 1)
    rows = [matrix[PANEL * k : PANEL * (k + 1), :] for k in range(count)]
    inverse = [(lane == place + PANEL * k).astype(F32) for k in range(count)]
    columns = {}
    for k in range(count):
        near = range(k, min(k + AHEAD, count))
        for i in near:
            if i not in columns:
                columns[i] = spread(rows[i], PANEL * k)
        later = {i: spread(rows[i], PANEL * (k + 1)) if k + 1 < count else [] for i in near}
        scale = jnp.zeros(shape, F32)
        for j in range(PANEL):
            root = lax.rsqrt(jnp.broadcast_to(columns[k][j][j : j + 1, :], shape))
            scale = jnp.where(place == j, root, scale)
            ratio = {i: columns[i][j] * (root * root) for i in near}
            ratio[k] = jnp.where(place > j, ratio[k], 0.0)
            row, unit = rows[k][j : j + 1, :], inverse[k][j : j + 1, :]
            now = [c[j : j + 1, :] for c in columns[k]]
            next_ = [c[j : j + 1, :] for c in later[k]]
            for i in near:
                rows[i] = rows[i] - ratio[i] * row
                inverse[i] = inverse[i] - ratio[i] * unit
                for l in range(j + 1, PANEL):
                    columns[i][l] = columns[i][l] - ratio[i] * now[l]
                later[i] = [c - ratio[i] * d for c, d in zip(later[i], next_)]
        rows[k] = jnp.where(lane >= place + PANEL * k, rows[k] * scale, 0.0)
        inverse[k] = inverse[k] * scale
        columns = {i: later[i] for i in near if i > k}
        if k + AHEAD < count:
            change = outer(rows[k], jnp.concatenate([rows[k], inverse[k]], axis=1))
            for i in range(k + AHEAD, count):
                at = slice(PANEL * i, PANEL * (i + 1))
                rows[i] = rows[i] - change[at, :width]
                inverse[i] = inverse[i] - change[at, width:]
    return jnp.concatenate(rows, axis=0), jnp.concatenate(inverse, axis=0)


def thirds(x):
    high = x.astype(jnp.bfloat16).astype(F32)
    rest = x - high
    middle = rest.astype(jnp.bfloat16).astype(F32)
    return high, middle, rest - middle


def outer(a, b):
    ah, am, al = thirds(a)
    bh, bm, bl = thirds(b)
    return lax.dot_general(
        jnp.concatenate([ah, ah, am, ah, am, al], axis=0).astype(jnp.bfloat16),
        jnp.concatenate([bh, bm, bh, bl, bm, bh], axis=0).astype(jnp.bfloat16),
        (((0,), (0,)), ((), ())),
        preferred_element_type=F32,
    )


def mm3(a, b, contract=(1, 0)):
    a_high, b_high = a.astype(jnp.bfloat16), b.astype(jnp.bfloat16)
    a_low = (a - a_high.astype(F32)).astype(jnp.bfloat16)
    b_low = (b - b_high.astype(F32)).astype(jnp.bfloat16)
    return lax.dot_general(
        jnp.concatenate([a_high, a_high, a_low], axis=contract[0]),
        jnp.concatenate([b_high, b_low, b_high], axis=contract[1]),
        (((contract[0],), (contract[1],)), ((), ())),
        preferred_element_type=F32,
    )


def finish_kernel(scale, pairs, sketch, basis, whole_r, one_r, upper_two, change_two):
    width = sketch.shape[1]
    chunks = [pairs[k : k + 2 * CHUNK, :] for k in range(0, 2 * width, 2 * CHUNK)]
    high = jnp.concatenate([c[:CHUNK] for c in chunks], axis=0)
    low = jnp.concatenate([c[CHUNK:] for c in chunks], axis=0)
    place = lax.broadcasted_iota(jnp.int32, (width, width), 0)
    lane = lax.broadcasted_iota(jnp.int32, (width, width), 1)
    eye = (place == lane).astype(F32)
    upper, inverse = factor(high)
    one_r[...] = upper / scale[0]
    basis_one = mm(sketch[...], inverse, (1, 1))
    flaw = mm(inverse, upper, (1, 1)) - eye
    parts = sliced(upper, 0, SLICES + 1)
    rest, carried = high, low
    for order in range(SLICES + 1):
        left = jnp.concatenate(parts[: order + 1], axis=0)
        right = jnp.concatenate(parts[: order + 1][::-1], axis=0)
        term = lax.dot_general(left, right, (((0,), (0,)), ((), ())), preferred_element_type=F32)
        rest, error = two_sum(rest, -term)
        carried = carried + error
    rest = rest + carried
    excess = mm3(mm3(inverse, rest), inverse, (1, 1)) + (flaw + flaw.T + mm3(flaw, flaw, (1, 1)))
    weight = jnp.where(place > lane, 1.0, jnp.where(place == lane, 0.5, 0.0))
    half = excess * weight
    square = mm3(half, half)
    sides = mm3(half, half, (1, 1))
    third = mm3(half, sides)
    left = (third + third.T) - (square + square.T + sides)
    last = left * weight
    change = mm3(last, half) - (half + last)
    change_two[...] = change
    lower_two = excess + change.T + mm3(excess, change, (1, 1))
    upper_two[...] = jnp.where(place <= lane, lower_two.T, 0.0)

    @pl.when(jnp.logical_not(jnp.sum(last * last) < 3e-7))
    def _():
        upper_full, inverse_full = factor(excess + eye)
        upper_two[...] = upper_full - eye
        change_two[...] = inverse_full - eye

    basis[...] = (basis_one + mm3(basis_one, change_two[...], (1, 1))) * scale[0]
    upper = upper - mm3(flaw, upper - mm3(flaw, upper, (0, 0)), (0, 0))
    whole_r[...] = (upper + mm3(upper_two[...], upper)) / scale[0]


def finish(pairs, sketch, scale):
    square = jax.ShapeDtypeStruct((sketch.shape[1],) * 2, F32)
    return pl.pallas_call(
        finish_kernel,
        out_shape=(jax.ShapeDtypeStruct(sketch.shape, F32), square, square),
        in_specs=[SMEM, VMEM, VMEM],
        out_specs=(VMEM, VMEM, VMEM),
        scratch_shapes=[pltpu.VMEM(square.shape, F32), pltpu.VMEM(square.shape, F32)],
        compiler_params=params(32),
        name="finish",
    )(scale.reshape(1), pairs, sketch)


def exchange(x, axes):
    return lax.all_to_all(x, axes, 0, 0, tiled=True)


def per_device(tile_values, tile_coords, tile_counts, omega):
    tile = tile_values.shape[2]
    width = omega.shape[1]
    partial = partial_sketch(tile_values, tile_coords, tile_counts, omega)
    got = lax.ppermute(partial[:HALF], "core", [(0, 1), (1, 0)])
    pieces = exchange(partial[HALF:RB] + got, "x")
    sketch, pairs = gram(pieces.reshape(4, HALF // 4 * tile, width))
    near, far = ("y", "x"), ("z", "core")
    pairs = add_pairs(exchange(pairs, near), 16)
    pairs = add_pairs(exchange(pairs, far), 32)
    pairs = exchange(pairs, near)
    total_rows = RB * tile * lax.axis_size(ROWS)
    return finish(pairs, sketch, jnp.sqrt(jnp.float32(total_rows)))


def solution(mesh):
    grid = Mesh(mesh.devices.reshape(8, 8, 4, 2), ("z", "y", "x", "core"))
    return jax.shard_map(
        per_device,
        mesh=grid,
        in_specs=(
            P(ROWS, COLUMNS, None),
            P(ROWS, COLUMNS),
            P(ROWS, COLUMNS),
            P(COLUMNS, None),
        ),
        out_specs=(P(ROWS + COLUMNS, None), P(), P()),
        check_vma=False,
    )
```

```python
import functools
import math

import jax
import jax.numpy as jnp
from jax import lax
from jax.experimental import pallas as pl
from jax.experimental.pallas import tpu as pltpu
from jax.sharding import Mesh, PartitionSpec as P

RB = 32
HALF = RB // 2
CHUNK = 4
PANEL = 8
AHEAD = 3
GROUP = 28
ROWS = "z", "y"
COLUMNS = "x", "core"
F32 = jnp.float32
HIGHEST = lax.Precision.HIGHEST
VMEM = pl.BlockSpec(memory_space=pltpu.VMEM)
SMEM = pl.BlockSpec(memory_space=pltpu.SMEM)
HBM = pl.BlockSpec(memory_space=pltpu.HBM)


def params(mib):
    return pltpu.CompilerParams(vmem_limit_bytes=mib * 2**20)


def mm(a, b, contract=(1, 0)):
    return lax.dot_general(
        a,
        b,
        (((contract[0],), (contract[1],)), ((), ())),
        precision=HIGHEST,
        preferred_element_type=F32,
    )


def two_sum(a, b):
    total = a + b
    other = total - a
    return total, (a - (total - other)) + (b - other)


def sketch_kernel(count, places, tiles, omega, total, held, blocks, products, coords, fetched, ready):
    tile = held.shape[1]
    used = count[0, 0]
    groups = lax.div(used + (GROUP - 1), GROUP)
    mine = lax.axis_index("core")

    def fetch(g):
        part = pl.ds(pl.multiple_of(g * GROUP, GROUP), GROUP)
        return pltpu.make_async_copy(tiles.at[part], held.at[part], fetched.at[g])

    first = [
        pltpu.make_async_copy(places, coords, ready.at[0]),
        pltpu.make_async_copy(omega, blocks, ready.at[1]),
    ]
    for copy in first:
        copy.start()

    @pl.loop(0, groups)
    def _(g):
        fetch(g).start()

    total[...] = jnp.zeros_like(total)
    for copy in first:
        copy.wait()

    @pl.loop(0, groups)
    def _(g):
        fetch(g).wait()
        for u in range(GROUP):
            s = g * GROUP + u
            column = jnp.clip(coords[1, s], 0, blocks.shape[0] // tile - 1)
            block = blocks[pl.ds(pl.multiple_of(column * tile, tile), tile), :]
            products[u] = jnp.dot(held[s], block, preferred_element_type=F32)
        for u in range(GROUP):
            s = g * GROUP + u
            row = coords[0, s]
            x, rest = lax.div(row, 8), lax.rem(row, 8)
            own = (lax.div(rest, 4) == mine).astype(jnp.int32)
            place = own * HALF + x * 4 + lax.rem(rest, 4)
            place = jnp.where(s < used, jnp.clip(place, 0, RB - 1), RB)
            total[place] += products[u]


def partial_sketch(tile_values, tile_coords, tile_counts, omega):
    slots, tile, _ = tile_values.shape
    width = omega.shape[1]
    return pl.pallas_call(
        sketch_kernel,
        out_shape=jax.ShapeDtypeStruct((RB + 1, tile, width), F32),
        in_specs=[SMEM, HBM, HBM, HBM],
        out_specs=VMEM,
        scratch_shapes=[
            pltpu.VMEM((slots, tile, tile), jnp.bfloat16),
            pltpu.VMEM(omega.shape, jnp.bfloat16),
            pltpu.VMEM((GROUP, tile, width), F32),
            pltpu.SMEM((2, slots), jnp.int32),
            pltpu.SemaphoreType.DMA((slots // GROUP,)),
            pltpu.SemaphoreType.DMA((2,)),
        ],
        compiler_params=params(32),
        name="sketch",
    )(
        tile_counts,
        pltpu.with_memory_space_constraint(tile_coords.T, pltpu.HBM),
        pltpu.with_memory_space_constraint(tile_values, pltpu.HBM),
        pltpu.with_memory_space_constraint(omega, pltpu.HBM),
    )


SLICES = 4
BITS = 8


def sliced(x, axis, count):
    grid = jnp.max(jnp.abs(x), axis=axis, keepdims=True) * (2.0**17)
    parts = []
    for _ in range(count):
        part = ((x + grid) - grid).astype(jnp.bfloat16)
        x = x - part.astype(F32)
        grid = grid * (2.0**-BITS)
        parts.append(part)
    return parts


def pair_of(orders):
    high, low = orders[0], jnp.zeros_like(orders[0])
    for term in orders[1:]:
        high, error = two_sum(high, term)
        low = low + error
    return two_sum(high, low)


def gram_kernel(pieces, sketch, pairs):
    rows, width = sketch.shape
    x = (pieces[0] + pieces[1]) + (pieces[2] + pieces[3])
    sketch[...] = x
    parts = sliced(x, 0, SLICES)
    across = jnp.concatenate(parts, axis=1)
    orders = [None] * (SLICES + 2)
    for i in range(SLICES):
        reach = min(SLICES, SLICES + 1 - i)
        block = lax.dot_general(
            parts[i],
            across[:, : reach * width],
            (((0,), (0,)), ((), ())),
            preferred_element_type=F32,
        )
        for j in range(reach):
            term = block[:, j * width : (j + 1) * width]
            o = i + j
            orders[o] = term if orders[o] is None else orders[o] + term
    high, low = pair_of([o for o in orders if o is not None])
    for k in range(width // CHUNK):
        at = slice(CHUNK * k, CHUNK * (k + 1))
        pairs[2 * CHUNK * k : 2 * CHUNK * (k + 1), :] = jnp.concatenate([high[at], low[at]], axis=0)


def gram(pieces):
    _, rows, width = pieces.shape
    return pl.pallas_call(
        gram_kernel,
        out_shape=(
            jax.ShapeDtypeStruct((rows, width), F32),
            jax.ShapeDtypeStruct((2 * width, width), F32),
        ),
        in_specs=[VMEM],
        out_specs=(VMEM, VMEM),
        compiler_params=params(32),
        name="gram",
    )(pieces)


def add_kernel(given, summed):
    step = 2 * CHUNK
    total, error = given[0:step, :], jnp.zeros((step, given.shape[1]), F32)
    for k in range(step, given.shape[0], step):
        total, slip = two_sum(total, given[k : k + step, :])
        error = error + slip
    high, low = two_sum(total[:CHUNK], total[CHUNK:] + error[:CHUNK])
    chunk = jnp.concatenate([high, low], axis=0)
    for k in range(0, summed.shape[0], step):
        summed[k : k + step, :] = chunk


def add_pairs(given, copies):
    return pl.pallas_call(
        add_kernel,
        out_shape=jax.ShapeDtypeStruct((2 * CHUNK * copies, given.shape[1]), F32),
        in_specs=[VMEM],
        out_specs=VMEM,
        compiler_params=params(16),
        name="add_pairs",
    )(given)


def spread(rows, at):
    return [jnp.broadcast_to(rows[:, at + j : at + j + 1], rows.shape) for j in range(PANEL)]


def factor(matrix):
    width = matrix.shape[0]
    count = width // PANEL
    shape = (PANEL, width)
    place = lax.broadcasted_iota(jnp.int32, shape, 0)
    lane = lax.broadcasted_iota(jnp.int32, shape, 1)
    rows = [matrix[PANEL * k : PANEL * (k + 1), :] for k in range(count)]
    inverse = [(lane == place + PANEL * k).astype(F32) for k in range(count)]
    columns = {}
    for k in range(count):
        near = range(k, min(k + AHEAD, count))
        for i in near:
            if i not in columns:
                columns[i] = spread(rows[i], PANEL * k)
        later = {i: spread(rows[i], PANEL * (k + 1)) if k + 1 < count else [] for i in near}
        scale = jnp.zeros(shape, F32)
        for j in range(PANEL):
            root = lax.rsqrt(jnp.broadcast_to(columns[k][j][j : j + 1, :], shape))
            scale = jnp.where(place == j, root, scale)
            ratio = {i: columns[i][j] * (root * root) for i in near}
            ratio[k] = jnp.where(place > j, ratio[k], 0.0)
            row, unit = rows[k][j : j + 1, :], inverse[k][j : j + 1, :]
            now = [c[j : j + 1, :] for c in columns[k]]
            next_ = [c[j : j + 1, :] for c in later[k]]
            for i in near:
                rows[i] = rows[i] - ratio[i] * row
                inverse[i] = inverse[i] - ratio[i] * unit
                for l in range(j + 1, PANEL):
                    columns[i][l] = columns[i][l] - ratio[i] * now[l]
                later[i] = [c - ratio[i] * d for c, d in zip(later[i], next_)]
        rows[k] = jnp.where(lane >= place + PANEL * k, rows[k] * scale, 0.0)
        inverse[k] = inverse[k] * scale
        columns = {i: later[i] for i in near if i > k}
        if k + AHEAD < count:
            change = outer(rows[k], jnp.concatenate([rows[k], inverse[k]], axis=1))
            for i in range(k + AHEAD, count):
                at = slice(PANEL * i, PANEL * (i + 1))
                rows[i] = rows[i] - change[at, :width]
                inverse[i] = inverse[i] - change[at, width:]
    return jnp.concatenate(rows, axis=0), jnp.concatenate(inverse, axis=0)


def thirds(x):
    high = x.astype(jnp.bfloat16).astype(F32)
    rest = x - high
    middle = rest.astype(jnp.bfloat16).astype(F32)
    return high, middle, rest - middle


def outer(a, b):
    ah, am, al = thirds(a)
    bh, bm, bl = thirds(b)
    return lax.dot_general(
        jnp.concatenate([ah, ah, am, ah, am, al], axis=0).astype(jnp.bfloat16),
        jnp.concatenate([bh, bm, bh, bl, bm, bh], axis=0).astype(jnp.bfloat16),
        (((0,), (0,)), ((), ())),
        preferred_element_type=F32,
    )


def mm3(a, b, contract=(1, 0)):
    a_high, b_high = a.astype(jnp.bfloat16), b.astype(jnp.bfloat16)
    a_low = (a - a_high.astype(F32)).astype(jnp.bfloat16)
    b_low = (b - b_high.astype(F32)).astype(jnp.bfloat16)
    return lax.dot_general(
        jnp.concatenate([a_high, a_high, a_low], axis=contract[0]),
        jnp.concatenate([b_high, b_low, b_high], axis=contract[1]),
        (((contract[0],), (contract[1],)), ((), ())),
        preferred_element_type=F32,
    )


def finish_kernel(scale, pairs, sketch, basis, whole_r, one_r, upper_two, change_two):
    width = sketch.shape[1]
    chunks = [pairs[k : k + 2 * CHUNK, :] for k in range(0, 2 * width, 2 * CHUNK)]
    high = jnp.concatenate([c[:CHUNK] for c in chunks], axis=0)
    low = jnp.concatenate([c[CHUNK:] for c in chunks], axis=0)
    place = lax.broadcasted_iota(jnp.int32, (width, width), 0)
    lane = lax.broadcasted_iota(jnp.int32, (width, width), 1)
    eye = (place == lane).astype(F32)
    upper, inverse = factor(high)
    one_r[...] = upper / scale
    basis_one = mm(sketch[...], inverse, (1, 1))
    flaw = mm(inverse, upper, (1, 1)) - eye
    parts = sliced(upper, 0, SLICES + 1)
    rest, carried = high, low
    for order in range(SLICES + 1):
        left = jnp.concatenate(parts[: order + 1], axis=0)
        right = jnp.concatenate(parts[: order + 1][::-1], axis=0)
        term = lax.dot_general(left, right, (((0,), (0,)), ((), ())), preferred_element_type=F32)
        rest, error = two_sum(rest, -term)
        carried = carried + error
    rest = rest + carried
    excess = mm3(mm3(inverse, rest), inverse, (1, 1)) + (flaw + flaw.T + mm3(flaw, flaw, (1, 1)))
    weight = jnp.where(place > lane, 1.0, jnp.where(place == lane, 0.5, 0.0))
    half = excess * weight
    square = mm3(half, half)
    sides = mm3(half, half, (1, 1))
    third = mm3(half, sides)
    left = (third + third.T) - (square + square.T + sides)
    last = left * weight
    change = mm3(last, half) - (half + last)
    change_two[...] = change
    lower_two = excess + change.T + mm3(excess, change, (1, 1))
    upper_two[...] = jnp.where(place <= lane, lower_two.T, 0.0)

    @pl.when(jnp.logical_not(jnp.sum(last * last) < 3e-7))
    def _():
        upper_full, inverse_full = factor(excess + eye)
        upper_two[...] = upper_full - eye
        change_two[...] = inverse_full - eye

    basis[...] = (basis_one + mm3(basis_one, change_two[...], (1, 1))) * scale
    upper = upper - mm3(flaw, upper - mm3(flaw, upper, (0, 0)), (0, 0))
    whole_r[...] = (upper + mm3(upper_two[...], upper)) / scale


def finish(pairs, sketch, scale):
    square = jax.ShapeDtypeStruct((sketch.shape[1],) * 2, F32)
    return pl.pallas_call(
        functools.partial(finish_kernel, scale),
        out_shape=(jax.ShapeDtypeStruct(sketch.shape, F32), square, square),
        in_specs=[VMEM, VMEM],
        out_specs=(VMEM, VMEM, VMEM),
        scratch_shapes=[pltpu.VMEM(square.shape, F32), pltpu.VMEM(square.shape, F32)],
        compiler_params=params(32),
        name="finish",
    )(pairs, sketch)


def exchange(x, axes):
    return lax.all_to_all(x, axes, 0, 0, tiled=True)


def per_device(tile_values, tile_coords, tile_counts, omega):
    tile = tile_values.shape[2]
    width = omega.shape[1]
    partial = partial_sketch(tile_values, tile_coords, tile_counts, omega)
    got = lax.ppermute(partial[:HALF], "core", [(0, 1), (1, 0)])
    pieces = exchange(partial[HALF:RB] + got, "x")
    sketch, pairs = gram(pieces.reshape(4, HALF // 4 * tile, width))
    near, far = ("y", "x"), ("z", "core")
    pairs = add_pairs(exchange(pairs, near), 16)
    pairs = add_pairs(exchange(pairs, far), 32)
    pairs = exchange(pairs, near)
    total_rows = RB * tile * lax.axis_size(ROWS)
    return finish(pairs, sketch, math.sqrt(total_rows))


def solution(mesh):
    grid = Mesh(mesh.devices.reshape(8, 8, 4, 2), ("z", "y", "x", "core"))
    return jax.shard_map(
        per_device,
        mesh=grid,
        in_specs=(
            P(ROWS, COLUMNS, None),
            P(ROWS, COLUMNS),
            P(ROWS, COLUMNS),
            P(COLUMNS, None),
        ),
        out_specs=(P(ROWS + COLUMNS, None), P(), P()),
        check_vma=False,
    )
```

```python
import functools
import math

import jax
import jax.numpy as jnp
from jax import lax
from jax.experimental import pallas as pl
from jax.experimental.pallas import tpu as pltpu
from jax.sharding import Mesh, PartitionSpec as P

RB = 32
HALF = RB // 2
CHUNK = 4
PANEL = 8
AHEAD = 3
GROUP = 28
ROWS = "z", "y"
COLUMNS = "x", "core"
F32 = jnp.float32
HIGHEST = lax.Precision.HIGHEST
VMEM = pl.BlockSpec(memory_space=pltpu.VMEM)
SMEM = pl.BlockSpec(memory_space=pltpu.SMEM)
HBM = pl.BlockSpec(memory_space=pltpu.HBM)


def params(mib):
    return pltpu.CompilerParams(vmem_limit_bytes=mib * 2**20)


def mm(a, b, contract=(1, 0)):
    return lax.dot_general(
        a,
        b,
        (((contract[0],), (contract[1],)), ((), ())),
        precision=HIGHEST,
        preferred_element_type=F32,
    )


def two_sum(a, b):
    total = a + b
    other = total - a
    return total, (a - (total - other)) + (b - other)


def sketch_kernel(count, places, tiles, omega, total, held, blocks, products, coords, fetched, ready):
    tile = held.shape[1]
    used = count[0, 0]
    groups = lax.div(used + (GROUP - 1), GROUP)
    mine = lax.axis_index("core")

    def fetch(g):
        part = pl.ds(pl.multiple_of(g * GROUP, GROUP), GROUP)
        return pltpu.make_async_copy(tiles.at[part], held.at[part], fetched.at[g])

    first = [
        pltpu.make_async_copy(places, coords, ready.at[0]),
        pltpu.make_async_copy(omega, blocks, ready.at[1]),
    ]
    for copy in first:
        copy.start()

    @pl.loop(0, groups)
    def _(g):
        fetch(g).start()

    total[...] = jnp.zeros_like(total)
    for copy in first:
        copy.wait()

    @pl.loop(0, groups)
    def _(g):
        fetch(g).wait()
        for u in range(GROUP):
            s = g * GROUP + u
            column = jnp.clip(coords[1, s], 0, blocks.shape[0] // tile - 1)
            block = blocks[pl.ds(pl.multiple_of(column * tile, tile), tile), :]
            products[u] = jnp.dot(held[s], block, preferred_element_type=F32)
        for u in range(GROUP):
            s = g * GROUP + u
            row = coords[0, s]
            x, rest = lax.div(row, 8), lax.rem(row, 8)
            own = (lax.div(rest, 4) == mine).astype(jnp.int32)
            place = own * HALF + x * 4 + lax.rem(rest, 4)
            place = jnp.where(s < used, jnp.clip(place, 0, RB - 1), RB)
            total[place] += products[u]


def partial_sketch(tile_values, tile_coords, tile_counts, omega):
    slots, tile, _ = tile_values.shape
    width = omega.shape[1]
    return pl.pallas_call(
        sketch_kernel,
        out_shape=jax.ShapeDtypeStruct((RB + 1, tile, width), F32),
        in_specs=[SMEM, HBM, HBM, HBM],
        out_specs=VMEM,
        scratch_shapes=[
            pltpu.VMEM((slots, tile, tile), jnp.bfloat16),
            pltpu.VMEM(omega.shape, jnp.bfloat16),
            pltpu.VMEM((GROUP, tile, width), F32),
            pltpu.SMEM((2, slots), jnp.int32),
            pltpu.SemaphoreType.DMA((slots // GROUP,)),
            pltpu.SemaphoreType.DMA((2,)),
        ],
        compiler_params=params(32),
        name="sketch",
    )(
        tile_counts,
        pltpu.with_memory_space_constraint(tile_coords.T, pltpu.HBM),
        pltpu.with_memory_space_constraint(tile_values, pltpu.HBM),
        pltpu.with_memory_space_constraint(omega, pltpu.HBM),
    )


SLICES = 4
BITS = 8


def sliced(x, axis, count):
    grid = jnp.max(jnp.abs(x), axis=axis, keepdims=True) * (2.0**17)
    parts = []
    for _ in range(count):
        part = ((x + grid) - grid).astype(jnp.bfloat16)
        x = x - part.astype(F32)
        grid = grid * (2.0**-BITS)
        parts.append(part)
    return parts


def pair_of(orders):
    high, low = orders[0], jnp.zeros_like(orders[0])
    for term in orders[1:]:
        high, error = two_sum(high, term)
        low = low + error
    return two_sum(high, low)


def gram_kernel(pieces, sketch, pairs):
    rows, width = sketch.shape
    x = (pieces[0] + pieces[1]) + (pieces[2] + pieces[3])
    sketch[...] = x
    parts = sliced(x, 0, SLICES)
    across = jnp.concatenate(parts, axis=1)
    orders = [None] * (SLICES + 2)
    for i in range(SLICES):
        reach = min(SLICES, SLICES + 1 - i)
        block = lax.dot_general(
            parts[i],
            across[:, : reach * width],
            (((0,), (0,)), ((), ())),
            preferred_element_type=F32,
        )
        for j in range(reach):
            term = block[:, j * width : (j + 1) * width]
            o = i + j
            orders[o] = term if orders[o] is None else orders[o] + term
    high, low = pair_of([o for o in orders if o is not None])
    for k in range(width // CHUNK):
        at = slice(CHUNK * k, CHUNK * (k + 1))
        pairs[2 * CHUNK * k : 2 * CHUNK * (k + 1), :] = jnp.concatenate([high[at], low[at]], axis=0)


def gram(pieces):
    _, rows, width = pieces.shape
    return pl.pallas_call(
        gram_kernel,
        out_shape=(
            jax.ShapeDtypeStruct((rows, width), F32),
            jax.ShapeDtypeStruct((2 * width, width), F32),
        ),
        in_specs=[VMEM],
        out_specs=(VMEM, VMEM),
        compiler_params=params(32),
        name="gram",
    )(pieces)


def add_kernel(given, summed):
    step = 2 * CHUNK
    total, error = given[0:step, :], jnp.zeros((step, given.shape[1]), F32)
    for k in range(step, given.shape[0], step):
        total, slip = two_sum(total, given[k : k + step, :])
        error = error + slip
    high, low = two_sum(total[:CHUNK], total[CHUNK:] + error[:CHUNK])
    chunk = jnp.concatenate([high, low], axis=0)
    for k in range(0, summed.shape[0], step):
        summed[k : k + step, :] = chunk


def add_pairs(given, copies):
    return pl.pallas_call(
        add_kernel,
        out_shape=jax.ShapeDtypeStruct((2 * CHUNK * copies, given.shape[1]), F32),
        in_specs=[VMEM],
        out_specs=VMEM,
        compiler_params=params(16),
        name="add_pairs",
    )(given)


def spread(rows, at):
    return [jnp.broadcast_to(rows[:, at + j : at + j + 1], rows.shape) for j in range(PANEL)]


def factor(matrix):
    width = matrix.shape[0]
    count = width // PANEL
    shape = (PANEL, width)
    place = lax.broadcasted_iota(jnp.int32, shape, 0)
    lane = lax.broadcasted_iota(jnp.int32, shape, 1)
    rows = [matrix[PANEL * k : PANEL * (k + 1), :] for k in range(count)]
    inverse = [(lane == place + PANEL * k).astype(F32) for k in range(count)]
    columns = {}
    for k in range(count):
        near = range(k, min(k + AHEAD, count))
        for i in near:
            if i not in columns:
                columns[i] = spread(rows[i], PANEL * k)
        later = {i: spread(rows[i], PANEL * (k + 1)) if k + 1 < count else [] for i in near}
        scale = jnp.zeros(shape, F32)
        for j in range(PANEL):
            root = lax.rsqrt(jnp.broadcast_to(columns[k][j][j : j + 1, :], shape))
            scale = jnp.where(place == j, root, scale)
            ratio = {i: columns[i][j] * (root * root) for i in near}
            ratio[k] = jnp.where(place > j, ratio[k], 0.0)
            row, unit = rows[k][j : j + 1, :], inverse[k][j : j + 1, :]
            now = [c[j : j + 1, :] for c in columns[k]]
            next_ = [c[j : j + 1, :] for c in later[k]]
            for i in near:
                rows[i] = rows[i] - ratio[i] * row
                inverse[i] = inverse[i] - ratio[i] * unit
                for l in range(j + 1, PANEL):
                    columns[i][l] = columns[i][l] - ratio[i] * now[l]
                later[i] = [c - ratio[i] * d for c, d in zip(later[i], next_)]
        rows[k] = jnp.where(lane >= place + PANEL * k, rows[k] * scale, 0.0)
        inverse[k] = inverse[k] * scale
        columns = {i: later[i] for i in near if i > k}
        if k + AHEAD < count:
            change = outer(rows[k], jnp.concatenate([rows[k], inverse[k]], axis=1))
            for i in range(k + AHEAD, count):
                at = slice(PANEL * i, PANEL * (i + 1))
                rows[i] = rows[i] - change[at, :width]
                inverse[i] = inverse[i] - change[at, width:]
    return jnp.concatenate(rows, axis=0), jnp.concatenate(inverse, axis=0)


def thirds(x):
    high = x.astype(jnp.bfloat16).astype(F32)
    rest = x - high
    middle = rest.astype(jnp.bfloat16).astype(F32)
    return high, middle, rest - middle


def outer(a, b):
    ah, am, al = thirds(a)
    bh, bm, bl = thirds(b)
    return lax.dot_general(
        jnp.concatenate([ah, ah, am, ah, am, al], axis=0).astype(jnp.bfloat16),
        jnp.concatenate([bh, bm, bh, bl, bm, bh], axis=0).astype(jnp.bfloat16),
        (((0,), (0,)), ((), ())),
        preferred_element_type=F32,
    )


def mm3(a, b, contract=(1, 0)):
    a_high, b_high = a.astype(jnp.bfloat16), b.astype(jnp.bfloat16)
    a_low = (a - a_high.astype(F32)).astype(jnp.bfloat16)
    b_low = (b - b_high.astype(F32)).astype(jnp.bfloat16)
    return lax.dot_general(
        jnp.concatenate([a_high, a_high, a_low], axis=contract[0]),
        jnp.concatenate([b_high, b_low, b_high], axis=contract[1]),
        (((contract[0],), (contract[1],)), ((), ())),
        preferred_element_type=F32,
    )


def finish_kernel(scale, pairs, sketch, basis, whole_r, one_r):
    width = sketch.shape[1]
    chunks = [pairs[k : k + 2 * CHUNK, :] for k in range(0, 2 * width, 2 * CHUNK)]
    high = jnp.concatenate([c[:CHUNK] for c in chunks], axis=0)
    low = jnp.concatenate([c[CHUNK:] for c in chunks], axis=0)
    place = lax.broadcasted_iota(jnp.int32, (width, width), 0)
    lane = lax.broadcasted_iota(jnp.int32, (width, width), 1)
    eye = (place == lane).astype(F32)
    upper, inverse = factor(high)
    one_r[...] = upper * (1.0 / scale)
    basis_one = mm(sketch[...], inverse, (1, 1))
    flaw = mm(inverse, upper, (1, 1)) - eye
    parts = sliced(upper, 0, SLICES + 1)
    rest, carried = high, low
    for order in range(SLICES + 1):
        left = jnp.concatenate(parts[: order + 1], axis=0)
        right = jnp.concatenate(parts[: order + 1][::-1], axis=0)
        term = lax.dot_general(left, right, (((0,), (0,)), ((), ())), preferred_element_type=F32)
        rest, error = two_sum(rest, -term)
        carried = carried + error
    rest = rest + carried
    excess = mm3(mm3(inverse, rest), inverse, (1, 1)) + (flaw + flaw.T + mm3(flaw, flaw, (1, 1)))
    weight = jnp.where(place > lane, 1.0, jnp.where(place == lane, 0.5, 0.0))
    half = excess * weight
    square = mm3(half, half)
    sides = mm3(half, half, (1, 1))
    third = mm3(half, sides)
    left = (third + third.T) - (square + square.T + sides)
    last = left * weight
    change = mm3(last, half) - (half + last)
    lower_two = excess + change.T + mm3(excess, change, (1, 1))
    upper_two = jnp.where(place <= lane, lower_two.T, 0.0)
    upper = upper - mm3(flaw, upper - mm3(flaw, upper, (0, 0)), (0, 0))

    def store(upper_two, change):
        basis[...] = (basis_one + mm3(basis_one, change, (1, 1))) * scale
        whole_r[...] = (upper + mm3(upper_two, upper)) * (1.0 / scale)

    store(upper_two, change)

    @pl.when(jnp.logical_not(jnp.sum(last * last) < 3e-7))
    def _():
        upper_full, inverse_full = factor(excess + eye)
        store(upper_full - eye, inverse_full - eye)


def finish(pairs, sketch, scale):
    square = jax.ShapeDtypeStruct((sketch.shape[1],) * 2, F32)
    return pl.pallas_call(
        functools.partial(finish_kernel, scale),
        out_shape=(jax.ShapeDtypeStruct(sketch.shape, F32), square, square),
        in_specs=[VMEM, VMEM],
        out_specs=(VMEM, VMEM, VMEM),
        compiler_params=params(32),
        name="finish",
    )(pairs, sketch)


def exchange(x, axes):
    return lax.all_to_all(x, axes, 0, 0, tiled=True)


def per_device(tile_values, tile_coords, tile_counts, omega):
    tile = tile_values.shape[2]
    width = omega.shape[1]
    partial = partial_sketch(tile_values, tile_coords, tile_counts, omega)
    got = lax.ppermute(partial[:HALF], "core", [(0, 1), (1, 0)])
    pieces = exchange(partial[HALF:RB] + got, "x")
    sketch, pairs = gram(pieces.reshape(4, HALF // 4 * tile, width))
    near, far = ("y", "x"), ("core", "z")
    pairs = add_pairs(exchange(pairs, near), 16)
    pairs = add_pairs(exchange(pairs, far), 32)
    pairs = exchange(pairs, near)
    total_rows = RB * tile * lax.axis_size(ROWS)
    return finish(pairs, sketch, math.sqrt(total_rows))


def solution(mesh):
    grid = Mesh(mesh.devices.reshape(8, 8, 4, 2), ("z", "y", "x", "core"))
    return jax.shard_map(
        per_device,
        mesh=grid,
        in_specs=(
            P(ROWS, COLUMNS, None),
            P(ROWS, COLUMNS),
            P(ROWS, COLUMNS),
            P(COLUMNS, None),
        ),
        out_specs=(P(ROWS + COLUMNS, None), P(), P()),
        check_vma=False,
    )
```
